512 devices in a mesh: mode: 64 (over y, z), real: 8 (over x, core).
Axes of the slice: x: 4, y: 8, z: 8, core: 2. Of those that a mesh axis runs over, the one named last changes fastest.
Arguments:
- input_field: bfloat16 [2, 8, 256, 16384], P(None, 'real', 'mode'), may hold values from -6 to 6
- kerr_coeff: bfloat16 [64, 64, 64], P('mode'), may hold values from -0.1875 to 0.1875
- block_list: int32 [64, 4], P('mode'), may hold values from 0 to 31
Outputs:
- density: float32 [512, 2, 256, 256], P('mode', None, 'real')
The draws below stay inside these ranges and needn't reach their ends.
All inputs are finite; a program needn't handle non-finite values.
Results may differ from the reference program's by a relative error of at most 0.0085.
Values may be sent and summed in bfloat16 or wider, within the bound.
No kernel may reach another device: no remote copies, remote signals or barrier semaphores. Data moves between devices by JAX's collectives and lax.ppermute only.
A program may use at most 64 MiB of HBM per device.

```python
import jax
import jax.numpy as jnp
from jax import lax

P_SIZE = 256
MB = 8
FT = 128
NB = 512
R_DEV = 1
NT = 16384
NMB = 32
FB = 32
NBLK = 64
RE = 8
N_REAL = 8


def with_ends(values, rng, smallest, top_value):
    longest = values.shape.index(max(values.shape))
    spots = []
    for shift in (0, 1):
        where = [jax.random.randint(jax.random.fold_in(rng, axis), (), 0, length) for axis, length in enumerate(values.shape)]
        where[longest] = (where[longest] + shift) % values.shape[longest]
        spots.append(tuple(where))
    return values.at[spots[0]].set(smallest).at[spots[1]].set(top_value)


def levels(stream_key, dims, split, least, largest):
    factor_of = 1.0
    for axis_at, parts in split:
        steps = jax.random.uniform(jax.random.fold_in(jax.random.fold_in(stream_key, 6), axis_at), (parts,), jnp.float32, least / len(split), largest / len(split))
        factor_of = factor_of * jnp.repeat(jnp.exp(steps), dims[axis_at] // parts).reshape((-1,) + (1,) * (len(dims) - 1 - axis_at))
    return factor_of


def normal_values(stream_key, shape, spread, limit, pieces=(), kind=jnp.bfloat16):
    drawn = spread * jax.random.normal(stream_key, shape, jnp.float32)
    if pieces:
        drawn = drawn * levels(stream_key, shape, pieces, -0.22, 0.18)
    return jnp.clip(drawn, -limit, limit).astype(kind)


def setup_inputs(seed: int = 0) -> dict:
    arg_keys = jax.random.split(jax.random.key(seed), 4)
    input_field = normal_values(arg_keys[0], (2, RE, P_SIZE, NT), 1.0, 6.0, ((1, 8), (2, 64)))
    kerr_coeff = normal_values(arg_keys[1], (NBLK, MB * MB, MB * MB), (16 * NBLK) ** -0.5, 0.1875, ((0, 64),))
    block_list = with_ends(jax.random.randint(arg_keys[2], (NBLK, 4), 0, NMB), jax.random.fold_in(arg_keys[2], 1), 0, NMB - 1).astype(jnp.int32)
    return dict(input_field=input_field, kerr_coeff=kerr_coeff, block_list=block_list)


kerr_strength = 0.25


def band_product(rows_part, cols_part):
    return jnp.einsum("rpbf,rqbf->bpq", rows_part.astype(jnp.float32), cols_part.astype(jnp.float32), precision=lax.Precision.HIGHEST)


def reference(input_field, kerr_coeff, block_list):
    total_real = R_DEV * N_REAL
    field_blocks = input_field.reshape(2, total_real, NMB, MB, NT)

    def add_block(running, item):
        coeff_one, block_one = item
        mode_l = lax.dynamic_index_in_dim(field_blocks, block_one[1], 2, keepdims=False).astype(jnp.float32)
        mode_m = lax.dynamic_index_in_dim(field_blocks, block_one[2], 2, keepdims=False).astype(jnp.float32)
        mode_n = lax.dynamic_index_in_dim(field_blocks, block_one[3], 2, keepdims=False).astype(jnp.float32)
        prod_re = mode_m[0][:, :, None, :] * mode_n[0][:, None, :, :] + mode_m[1][:, :, None, :] * mode_n[1][:, None, :, :]
        prod_im = mode_m[1][:, :, None, :] * mode_n[0][:, None, :, :] - mode_m[0][:, :, None, :] * mode_n[1][:, None, :, :]
        pairs = jnp.stack([prod_re, prod_im]).reshape(2, total_real, MB * MB, NT).astype(jnp.bfloat16)
        weighted = jnp.einsum("ab,crbt->crat", coeff_one.astype(jnp.float32), pairs.astype(jnp.float32), precision=lax.Precision.HIGHEST)
        weighted = weighted.reshape(2, total_real, MB, MB, NT)
        term_re = jnp.sum(weighted[0] * mode_l[0][:, None] - weighted[1] * mode_l[1][:, None], axis=2)
        term_im = jnp.sum(weighted[0] * mode_l[1][:, None] + weighted[1] * mode_l[0][:, None], axis=2)
        target = block_one[0]
        before = lax.dynamic_index_in_dim(running, target, 2, keepdims=False)
        running = lax.dynamic_update_index_in_dim(running, before + jnp.stack([term_re, term_im]), target, 2)
        return running, None

    initial = jnp.zeros((2, total_real, NMB, MB, NT), jnp.float32)
    kerr_sum, unused = lax.scan(add_block, initial, (kerr_coeff, block_list))
    kerr_sum = kerr_sum.reshape(2, total_real, P_SIZE, NT)
    base = input_field.astype(jnp.float32)
    stepped_re = (base[0] - kerr_strength * kerr_sum[1]).astype(jnp.bfloat16)
    stepped_im = (base[1] + kerr_strength * kerr_sum[0]).astype(jnp.bfloat16)
    spectrum = jnp.fft.fft(lax.complex(stepped_re.astype(jnp.float32), stepped_im.astype(jnp.float32)), axis=-1) / FT
    spec_re = lax.optimization_barrier(jnp.real(spectrum).astype(jnp.bfloat16))
    spec_im = lax.optimization_barrier(jnp.imag(spectrum).astype(jnp.bfloat16))
    band_re = spec_re.reshape(total_real, P_SIZE, NB, FB)
    band_im = spec_im.reshape(total_real, P_SIZE, NB, FB)
    dens_re = band_product(band_re, band_re) + band_product(band_im, band_im)
    dens_im = band_product(band_im, band_re) - band_product(band_re, band_im)
    return jnp.stack([dens_re, dens_im], axis=1) / (FB * total_real)
```

```python
import math

import jax
import jax.numpy as jnp
import numpy as np
from jax import lax
from jax.experimental import pallas as pl
from jax.experimental.pallas import tpu as pltpu
from jax.sharding import Mesh
from jax.sharding import PartitionSpec as P

MB = 8
FT = 128
FB = 32
NMB = 32
NBLK = 64
MODES = 256
NDEV = 64
MODE = ("y", "z")
F32 = jnp.float32
BF16 = jnp.bfloat16

kerr_strength = 0.25

VMEM_LIMIT = 48 * 2**20


def params():
    return pltpu.CompilerParams(vmem_limit_bytes=VMEM_LIMIT)


def in_vmem():
    return pl.BlockSpec(memory_space=pltpu.VMEM)


def in_smem():
    return pl.BlockSpec(memory_space=pltpu.SMEM)


def pack_kernel(core_ref, list_ref, field_ref, coeff_ref, out_ref):
    core = core_ref[0]
    row = lax.broadcasted_iota(jnp.int32, (32, 64), 0) + 32 * core
    col = lax.broadcasted_iota(jnp.int32, (32, 64), 1)
    pick = (col == (row % MB) * MB + row // MB).astype(F32).astype(BF16)
    own = jnp.dot(pick, coeff_ref[0], preferred_element_type=F32)
    own = jnp.concatenate([own[:16], own[16:]], axis=1).astype(BF16)
    lane = lax.broadcasted_iota(jnp.int32, (8, 128), 1)
    index = jnp.zeros((8, 128), jnp.int32)
    for j in range(4):
        index = jnp.where(lane == j, list_ref[0, j], index)
    index = index.astype(F32).astype(BF16)
    for i in range(NDEV):
        pieces = []
        for tt in range(2):
            for part in range(2):
                pieces.append(
                    field_ref[part, 0, :, pl.ds((2 * i + tt) * 128, 128)].astype(F32)
                )
        out_ref[i, 0:16, :] = jnp.concatenate(pieces, axis=0).astype(BF16)
        out_ref[i, 16:32, :] = own
        out_ref[i, 32:40, :] = index


def pack(core, block_list, field, coeff):
    return pl.pallas_call(
        pack_kernel,
        out_shape=jax.ShapeDtypeStruct((NDEV, 40, 128), BF16),
        in_specs=[in_smem(), in_smem(), in_vmem(), in_vmem()],
        out_specs=in_vmem(),
        compiler_params=params(),
        name="pack",
    )(core, block_list, field, coeff)


def kerr_kernel(list_ref, data_ref, coeff_ref, out_ref, field, total):
    for b in range(NMB):
        first = data_ref[2 * b, 0:16, :].astype(F32)
        second = data_ref[2 * b + 1, 0:16, :].astype(F32)
        for tt in range(2):
            for part in range(2):
                at = 8 * tt + 4 * part
                field[part, b, :, tt * 128 : tt * 128 + 128] = jnp.concatenate(
                    [first[at : at + 4], second[at : at + 4]], axis=0
                )
    total[...] = jnp.zeros(total.shape, F32)

    def one_block(k, carry):
        at_p = list_ref[k, 0]
        at_l = list_ref[k, 1]
        at_m = list_ref[k, 2]
        at_n = list_ref[k, 3]
        n_re = field[0, at_n]
        n_im = field[1, at_n]
        pair_re = []
        pair_im = []
        for m in range(MB):
            m_re = field[0, at_m, m : m + 1, :]
            m_im = field[1, at_m, m : m + 1, :]
            pair_re.append(m_re * n_re + m_im * n_im)
            pair_im.append(m_im * n_re - m_re * n_im)
        pairs = jnp.concatenate(
            [jnp.concatenate(pair_re, axis=0), jnp.concatenate(pair_im, axis=0)], axis=1
        ).astype(BF16)
        low = coeff_ref[0, k]
        high = coeff_ref[1, k]
        table = jnp.concatenate(
            [low[:, :64], low[:, 64:], high[:, :64], high[:, 64:]], axis=0
        )
        weighted = jnp.dot(table, pairs, preferred_element_type=F32)
        term_re = jnp.zeros((MB, 256), F32)
        term_im = jnp.zeros((MB, 256), F32)
        for l in range(MB):
            w_re = weighted[8 * l : 8 * l + 8, :256]
            w_im = weighted[8 * l : 8 * l + 8, 256:]
            l_re = field[0, at_l, l : l + 1, :]
            l_im = field[1, at_l, l : l + 1, :]
            term_re = term_re + (w_re * l_re - w_im * l_im)
            term_im = term_im + (w_re * l_im + w_im * l_re)
        total[0, at_p] += term_re
        total[1, at_p] += term_im
        return carry

    lax.fori_loop(0, NBLK, one_block, 0, unroll=2)

    for b in range(NMB):
        new_re = field[0, b] - kerr_strength * total[1, b]
        new_im = field[1, b] + kerr_strength * total[0, b]
        new = (new_re, new_im)
        for half in range(2):
            pieces = []
            for tt in range(2):
                for part in range(2):
                    pieces.append(
                        new[part][4 * half : 4 * half + 4, tt * 128 : tt * 128 + 128]
                    )
            out_ref[2 * b + half] = jnp.concatenate(pieces, axis=0).astype(BF16)


def kerr_step(block_list, data, coeff):
    return pl.pallas_call(
        kerr_kernel,
        out_shape=jax.ShapeDtypeStruct((NDEV, 16, 128), BF16),
        in_specs=[in_smem(), in_vmem(), in_vmem()],
        out_specs=in_vmem(),
        scratch_shapes=[
            pltpu.VMEM((2, NMB, MB, 256), F32),
            pltpu.VMEM((2, NMB, MB, 256), F32),
        ],
        compiler_params=params(),
        name="kerr",
    )(block_list, data, coeff)


def dft_tables():
    a = np.arange(FT)
    angle = 2.0 * math.pi / FT * ((a[:, None] * a[None, :]) % FT)
    cos, sin = np.cos(angle), -np.sin(angle)
    first = np.block([[cos, -sin], [sin, cos]])
    small = 2.0 * math.pi / (FT * FT) * (a[:, None] * a[None, :])
    twist = np.stack([np.cos(small), -np.sin(small)])
    return (
        jnp.asarray(first, BF16),
        jnp.asarray(first / FT, BF16),
        jnp.asarray(twist, F32),
    )


def dft_kernel(first_ref, second_ref, twist_ref, data_ref, out_ref, rows):
    rows[...] = data_ref[...].astype(F32).reshape(1024, 128)
    columns = []
    for m in range(4):
        columns.append(
            jnp.concatenate(
                [rows[pl.ds(m, 128, stride=8), :], rows[pl.ds(4 + m, 128, stride=8), :]],
                axis=0,
            ).astype(BF16)
        )
    half = jnp.dot(
        first_ref[...], jnp.concatenate(columns, axis=1), preferred_element_type=F32
    )
    t_re = twist_ref[0]
    t_im = twist_ref[1]
    turned = []
    for m in range(4):
        h_re = half[:128, 128 * m : 128 * m + 128]
        h_im = half[128:, 128 * m : 128 * m + 128]
        turned.append(
            jnp.concatenate(
                [h_re * t_re - h_im * t_im, h_re * t_im + h_im * t_re], axis=1
            ).astype(BF16)
        )
    spectrum = lax.dot_general(
        second_ref[...],
        jnp.concatenate(turned, axis=0),
        (((1,), (1,)), ((), ())),
        preferred_element_type=F32,
    )
    for part in range(2):
        for m in range(4):
            rows[pl.ds(4 * part + m, 128, stride=8), :] = spectrum[
                128 * part : 128 * part + 128, 128 * m : 128 * m + 128
            ]
    out_ref[...] = rows[...].reshape(NDEV, 16, 128).astype(BF16)


def transform(data):
    first, second, twist = dft_tables()
    return pl.pallas_call(
        dft_kernel,
        out_shape=jax.ShapeDtypeStruct((NDEV, 16, 128), BF16),
        in_specs=[in_vmem()] * 4,
        out_specs=in_vmem(),
        scratch_shapes=[pltpu.VMEM((1024, 128), F32)],
        compiler_params=params(),
        name="dft",
    )(first, second, twist, data)


def order_kernel(data_ref, out_ref):
    for b in range(MODES // 16):
        group = [data_ref[4 * b + s].astype(F32) for s in range(4)]
        for h in range(2):
            for part in range(2):
                at = 8 * h + 4 * part
                piece = jnp.concatenate([g[at : at + 4] for g in group], axis=0).astype(BF16)
                for copy in range(4):
                    out_ref[copy, h, part, 16 * b : 16 * b + 16, :] = piece


def order(data):
    return pl.pallas_call(
        order_kernel,
        out_shape=jax.ShapeDtypeStruct((4, 2, 2, MODES, 128), BF16),
        in_specs=[in_vmem()],
        out_specs=in_vmem(),
        compiler_params=params(),
        name="order",
    )(data)


def gram_kernel(first_ref, own_ref, other_ref, out_ref):
    start = pl.multiple_of(first_ref[0], 32)
    lane = lax.broadcasted_iota(jnp.int32, (32, 128), 1) // FB
    for h in range(2):
        lefts = [[] for _ in range(8)]
        rights = []
        for data_ref in (own_ref, other_ref):
            for x in range(4):
                re = data_ref[x, h, 0]
                im = data_ref[x, h, 1]
                rights += [re, im]
                own_re = data_ref[x, h, 0, pl.ds(start, 32), :].astype(F32)
                own_im = data_ref[x, h, 1, pl.ds(start, 32), :].astype(F32)
                for band in range(4):
                    b_re = jnp.where(lane == band, own_re, 0.0)
                    b_im = jnp.where(lane == band, own_im, 0.0)
                    lefts[2 * band] += [b_re.astype(BF16), b_im.astype(BF16)]
                    lefts[2 * band + 1] += [b_im.astype(BF16), (-b_re).astype(BF16)]
        left = jnp.concatenate([jnp.concatenate(p, axis=1) for p in lefts], axis=0)
        right = jnp.concatenate(rights, axis=1)
        result = lax.dot_general(
            left, right, (((1,), (1,)), ((), ())), preferred_element_type=F32
        ) * (1.0 / 256.0)
        for band in range(4):
            for d in range(2):
                at = 64 * band + 32 * d
                out_ref[4 * h + band, d] = result[at : at + 32]


def gram(first_row, own, other):
    return pl.pallas_call(
        gram_kernel,
        out_shape=jax.ShapeDtypeStruct((8, 2, 32, MODES), F32),
        in_specs=[in_smem(), in_vmem(), in_vmem()],
        out_specs=in_vmem(),
        compiler_params=params(),
        name="gram",
    )(first_row, own, other)


def swap(array, axes):
    return lax.all_to_all(array, axes, split_axis=0, concat_axis=0, tiled=True)


def shards(input_field, kerr_coeff, block_list):
    core = lax.axis_index("c")
    chip = lax.axis_index("x")
    packed = pack(core.reshape(1), block_list, input_field, kerr_coeff)
    timed = swap(packed, MODE)
    coeff = lax.all_gather(timed[:, 16:32, :], "c", axis=0, tiled=False)
    indices = timed[:, 32, 0:4].astype(jnp.int32)
    stepped = kerr_step(indices, timed, coeff)
    spectrum = transform(swap(stepped, MODE))
    banded = order(swap(spectrum, MODE))
    own = swap(banded, ("x",))
    other = lax.ppermute(own, "c", ((0, 1), (1, 0)))
    first_row = (2 * chip + core) * 32
    return gram(first_row.reshape(1), own, other)


def solution(mesh):
    finer = Mesh(mesh.devices.reshape(8, 8, 4, 2), ("y", "z", "x", "c"))
    return jax.shard_map(
        shards,
        mesh=finer,
        in_specs=(P(None, ("x", "c"), MODE, None), P(MODE, None, None), P(MODE, None)),
        out_specs=P(MODE, None, ("x", "c"), None),
        check_vma=False,
    )
```

```python
import math

import jax
import jax.numpy as jnp
import numpy as np
from jax import lax
from jax.experimental import pallas as pl
from jax.experimental.pallas import tpu as pltpu
from jax.sharding import Mesh
from jax.sharding import PartitionSpec as P

MB = 8
FT = 128
FB = 32
NMB = 32
NBLK = 64
MODES = 256
NDEV = 64
MODE = ("y", "z")
F32 = jnp.float32
BF16 = jnp.bfloat16

kerr_strength = 0.25

VMEM_LIMIT = 48 * 2**20


def params(limit=VMEM_LIMIT):
    return pltpu.CompilerParams(vmem_limit_bytes=limit)


def in_vmem():
    return pl.BlockSpec(memory_space=pltpu.VMEM)


def in_hbm():
    return pl.BlockSpec(memory_space=pltpu.HBM)


def in_smem():
    return pl.BlockSpec(memory_space=pltpu.SMEM)


def pack_kernel(place_ref, list_ref, field_hbm, coeff_hbm, out_ref, field, coeff, sems):
    field_copy = pltpu.make_async_copy(field_hbm, field, sems.at[0])
    coeff_copy = pltpu.make_async_copy(coeff_hbm, coeff, sems.at[1])
    field_copy.start()
    coeff_copy.start()
    core = place_ref[0]
    row = lax.broadcasted_iota(jnp.int32, (32, 64), 0) + 32 * core
    col = lax.broadcasted_iota(jnp.int32, (32, 64), 1)
    pick = (col == (row % MB) * MB + row // MB).astype(F32).astype(BF16)
    lane = lax.broadcasted_iota(jnp.int32, (4, 128), 1)
    line = lax.broadcasted_iota(jnp.int32, (4, 128), 0)
    index = jnp.zeros((4, 128), jnp.int32)
    for j in range(4):
        index = jnp.where((lane == place_ref[1]) & (line == j), list_ref[0, j], index)
    index = index.astype(F32).astype(BF16)
    coeff_copy.wait()
    own = jnp.dot(pick, coeff[0], preferred_element_type=F32)
    own = jnp.concatenate([own[:16], own[16:]], axis=1).astype(BF16)
    for i in range(NDEV):
        for q in range(4):
            out_ref[i, 4 + q] = own[4 * q : 4 * q + 4]
        out_ref[i, 8] = index
    field_copy.wait()
    for i in range(NDEV):
        for tt in range(2):
            for part in range(2):
                out_ref[i, 2 * tt + part] = field[
                    part, 0, :, (2 * i + tt) * 128 : (2 * i + tt) * 128 + 128
                ]


def pack(place, block_list, field, coeff):
    return pl.pallas_call(
        pack_kernel,
        out_shape=jax.ShapeDtypeStruct((NDEV, 9, 4, 128), BF16),
        in_specs=[in_smem(), in_smem(), in_hbm(), in_hbm()],
        out_specs=in_vmem(),
        scratch_shapes=[
            pltpu.VMEM(field.shape, BF16),
            pltpu.VMEM(coeff.shape, BF16),
            pltpu.SemaphoreType.DMA((2,)),
        ],
        compiler_params=params(60 * 2**20),
        name="pack",
    )(place, block_list, field, coeff)


def kerr_kernel(data_ref, coeff_ref, out_ref, field, total, listed, indices, sem):
    index = jnp.sum(data_ref[:, 8].astype(F32), axis=0)
    listed[...] = jnp.concatenate([index, index], axis=0).astype(jnp.int32)
    list_copy = pltpu.make_async_copy(listed, indices, sem)
    list_copy.start()
    for b in range(NMB):
        for tt in range(2):
            for part in range(2):
                both = jnp.concatenate(
                    [
                        data_ref[2 * b, 2 * tt + part].astype(F32),
                        data_ref[2 * b + 1, 2 * tt + part].astype(F32),
                    ],
                    axis=0,
                )
                field[part, b, :, tt * 128 : tt * 128 + 128] = both
                total[part, b, :, tt * 128 : tt * 128 + 128] = both
    list_copy.wait()

    def one_block(k, carry):
        at_p = indices[0, k]
        at_l = indices[1, k]
        at_m = indices[2, k]
        at_n = indices[3, k]
        n_re = field[0, at_n]
        n_im = field[1, at_n]
        pair_re = []
        pair_im = []
        for m in range(MB):
            m_re = field[0, at_m, m : m + 1, :]
            m_im = field[1, at_m, m : m + 1, :]
            pair_re.append(m_re * n_re + m_im * n_im)
            pair_im.append(m_im * n_re - m_re * n_im)
        pairs = jnp.concatenate(
            [jnp.concatenate(pair_re, axis=0), jnp.concatenate(pair_im, axis=0)], axis=1
        ).astype(BF16)
        low = coeff_ref[0, k]
        high = coeff_ref[1, k]
        table = jnp.concatenate(
            [low[:, :64], low[:, 64:], high[:, :64], high[:, 64:]], axis=0
        )
        weighted = jnp.dot(table, pairs, preferred_element_type=F32)
        term_re = jnp.zeros((MB, 256), F32)
        term_im = jnp.zeros((MB, 256), F32)
        for l in range(MB):
            w_re = weighted[8 * l : 8 * l + 8, :256]
            w_im = weighted[8 * l : 8 * l + 8, 256:]
            l_re = field[0, at_l, l : l + 1, :]
            l_im = field[1, at_l, l : l + 1, :]
            term_re = term_re + (w_re * l_re - w_im * l_im)
            term_im = term_im + (w_re * l_im + w_im * l_re)
        total[0, at_p] -= kerr_strength * term_im
        total[1, at_p] += kerr_strength * term_re
        return carry

    lax.fori_loop(0, NBLK, one_block, 0, unroll=16)

    for b in range(NMB):
        new = (total[0, b], total[1, b])
        for half in range(2):
            pieces = []
            for tt in range(2):
                for part in range(2):
                    pieces.append(
                        new[part][4 * half : 4 * half + 4, tt * 128 : tt * 128 + 128]
                    )
            out_ref[2 * b + half] = jnp.concatenate(pieces, axis=0).astype(BF16)


def kerr_step(data, coeff):
    return pl.pallas_call(
        kerr_kernel,
        out_shape=jax.ShapeDtypeStruct((NDEV, 16, 128), BF16),
        in_specs=[in_vmem(), in_vmem()],
        out_specs=in_vmem(),
        scratch_shapes=[
            pltpu.VMEM((2, NMB, MB, 256), F32),
            pltpu.VMEM((2, NMB, MB, 256), F32),
            pltpu.VMEM((8, 128), jnp.int32),
            pltpu.SMEM((8, 128), jnp.int32),
            pltpu.SemaphoreType.DMA,
        ],
        compiler_params=params(),
        name="kerr",
    )(data, coeff)


def dft_tables():
    a = np.arange(FT)
    angle = 2.0 * math.pi / FT * ((a[:, None] * a[None, :]) % FT)
    cos, sin = np.cos(angle), -np.sin(angle)
    first = np.block([[cos, -sin], [sin, cos]])
    small = 2.0 * math.pi / (FT * FT) * (a[:, None] * a[None, :])
    twist = np.stack([np.cos(small), -np.sin(small)])
    return (
        jnp.asarray(first, BF16),
        jnp.asarray(first / FT, BF16),
        jnp.asarray(twist, F32),
    )


def dft_kernel(first_ref, second_ref, twist_ref, data_ref, out_ref, rows):
    rows[...] = data_ref[...].astype(F32).reshape(1024, 128)
    columns = []
    for m in range(4):
        columns.append(
            jnp.concatenate(
                [rows[pl.ds(m, 128, stride=8), :], rows[pl.ds(4 + m, 128, stride=8), :]],
                axis=0,
            ).astype(BF16)
        )
    half = jnp.dot(
        first_ref[...], jnp.concatenate(columns, axis=1), preferred_element_type=F32
    )
    t_re = twist_ref[0]
    t_im = twist_ref[1]
    turned = []
    for m in range(4):
        h_re = half[:128, 128 * m : 128 * m + 128]
        h_im = half[128:, 128 * m : 128 * m + 128]
        turned.append(
            jnp.concatenate(
                [h_re * t_re - h_im * t_im, h_re * t_im + h_im * t_re], axis=1
            ).astype(BF16)
        )
    spectrum = lax.dot_general(
        second_ref[...],
        jnp.concatenate(turned, axis=0),
        (((1,), (1,)), ((), ())),
        preferred_element_type=F32,
    )
    for part in range(2):
        for m in range(4):
            rows[pl.ds(4 * part + m, 128, stride=8), :] = spectrum[
                128 * part : 128 * part + 128, 128 * m : 128 * m + 128
            ]
    out_ref[...] = rows[...].reshape(NDEV, 16, 128).astype(BF16)


def transform(data):
    first, second, twist = dft_tables()
    return pl.pallas_call(
        dft_kernel,
        out_shape=jax.ShapeDtypeStruct((NDEV, 16, 128), BF16),
        in_specs=[in_vmem()] * 4,
        out_specs=in_vmem(),
        scratch_shapes=[pltpu.VMEM((1024, 128), F32)],
        compiler_params=params(),
        name="dft",
    )(first, second, twist, data)


def order_kernel(data_ref, out_ref):
    for b in range(MODES // 16):
        group = [data_ref[4 * b + s].astype(F32) for s in range(4)]
        for h in range(2):
            for part in range(2):
                at = 8 * h + 4 * part
                piece = jnp.concatenate([g[at : at + 4] for g in group], axis=0).astype(BF16)
                for copy in range(4):
                    out_ref[copy, h, part, 16 * b : 16 * b + 16, :] = piece


def order(data):
    return pl.pallas_call(
        order_kernel,
        out_shape=jax.ShapeDtypeStruct((4, 2, 2, MODES, 128), BF16),
        in_specs=[in_vmem()],
        out_specs=in_vmem(),
        compiler_params=params(),
        name="order",
    )(data)


def gram_kernel(place_ref, data_ref, own_ref, send_ref):
    core = place_ref[0]
    keep = pl.multiple_of(64 * place_ref[2] + 32 * core, 32)
    give = pl.multiple_of(64 * place_ref[2] + 32 * (1 - core), 32)
    lane = lax.broadcasted_iota(jnp.int32, (32, 128), 1) // FB
    for h in range(2):
        lefts = [[] for _ in range(16)]
        rights = []
        for x in range(4):
            rights += [data_ref[x, h, 0], data_ref[x, h, 1]]
            for side, start in enumerate((keep, give)):
                row_re = data_ref[x, h, 0, pl.ds(start, 32), :].astype(F32)
                row_im = data_ref[x, h, 1, pl.ds(start, 32), :].astype(F32)
                for band in range(4):
                    b_re = jnp.where(lane == band, row_re, 0.0)
                    b_im = jnp.where(lane == band, row_im, 0.0)
                    at = 8 * side + 2 * band
                    lefts[at] += [b_re.astype(BF16), b_im.astype(BF16)]
                    lefts[at + 1] += [b_im.astype(BF16), (-b_re).astype(BF16)]
        left = jnp.concatenate([jnp.concatenate(p, axis=1) for p in lefts], axis=0)
        right = jnp.concatenate(rights, axis=1)
        result = lax.dot_general(
            left, right, (((1,), (1,)), ((), ())), preferred_element_type=F32
        ) * (1.0 / 256.0)
        for band in range(4):
            for d in range(2):
                at = 64 * band + 32 * d
                own_ref[4 * h + band, d] = result[at : at + 32]
                send_ref[4 * h + band, d] = result[256 + at : 256 + at + 32].astype(BF16)


def gram(place, data):
    return pl.pallas_call(
        gram_kernel,
        out_shape=(
            jax.ShapeDtypeStruct((8, 2, 32, MODES), F32),
            jax.ShapeDtypeStruct((8, 2, 32, MODES), BF16),
        ),
        in_specs=[in_smem(), in_vmem()],
        out_specs=(in_vmem(), in_vmem()),
        compiler_params=params(),
        name="gram",
    )(place, data)


def add_kernel(place_ref, own_ref, sent_ref, out_ref):
    out_ref[...] = own_ref[...] + sent_ref[1 - place_ref[0]].astype(F32)


def add(place, own, sent):
    return pl.pallas_call(
        add_kernel,
        out_shape=jax.ShapeDtypeStruct((8, 2, 32, MODES), F32),
        in_specs=[in_smem(), in_vmem(), in_vmem()],
        out_specs=in_vmem(),
        compiler_params=params(),
        name="add",
    )(place, own, sent)


def swap(array, axes):
    return lax.all_to_all(array, axes, split_axis=0, concat_axis=0, tiled=True)


def shards(input_field, kerr_coeff, block_list):
    place = jnp.stack([lax.axis_index("c"), lax.axis_index(MODE), lax.axis_index("x")])
    timed = swap(pack(place, block_list, input_field, kerr_coeff), MODE)
    halves = timed[:, 4:8].reshape(NDEV, 16, 128)
    coeff = lax.all_gather(halves, "c", axis=0, tiled=False)
    stepped = kerr_step(timed, coeff)
    spectrum = transform(swap(stepped, MODE))
    banded = order(swap(spectrum, MODE))
    own, send = gram(place, swap(banded, ("x",)))
    return add(place, own, lax.all_gather(send, "c", axis=0, tiled=False))


def solution(mesh):
    finer = Mesh(mesh.devices.reshape(8, 8, 4, 2), ("y", "z", "x", "c"))
    return jax.shard_map(
        shards,
        mesh=finer,
        in_specs=(P(None, ("x", "c"), MODE, None), P(MODE, None, None), P(MODE, None)),
        out_specs=P(MODE, None, ("x", "c"), None),
        check_vma=False,
    )
```

```python
import math

import jax
import jax.numpy as jnp
import numpy as np
from jax import lax
from jax.experimental import pallas as pl
from jax.experimental.pallas import tpu as pltpu
from jax.sharding import Mesh
from jax.sharding import PartitionSpec as P

MB = 8
FT = 128
FB = 32
NT = 16384
PACK_PARTS = 4
NMB = 32
NBLK = 64
MODES = 256
NDEV = 64
MODE = ("y", "z")
F32 = jnp.float32
BF16 = jnp.bfloat16

kerr_strength = 0.25

VMEM_LIMIT = 48 * 2**20


def params(limit=VMEM_LIMIT):
    return pltpu.CompilerParams(vmem_limit_bytes=limit)


def in_vmem():
    return pl.BlockSpec(memory_space=pltpu.VMEM)


def in_hbm():
    return pl.BlockSpec(memory_space=pltpu.HBM)


def pack_kernel(list_hbm, field_hbm, coeff_hbm, out_hbm, listed, field, coeff, out, sems, out_sems):
    coeff_copy = pltpu.make_async_copy(coeff_hbm, coeff, sems.at[0])
    list_copy = pltpu.make_async_copy(list_hbm, listed, sems.at[1])
    coeff_copy.start()
    list_copy.start()
    field_copies = []
    for g in range(PACK_PARTS):
        times = pl.ds(g * (NT // PACK_PARTS), NT // PACK_PARTS)
        field_copies.append(
            pltpu.make_async_copy(
                field_hbm.at[:, :, :, times], field.at[:, :, :, times], sems.at[2 + g]
            )
        )
        field_copies[g].start()
    core = lax.axis_index("c")
    place = lax.axis_index(MODE)
    row = lax.broadcasted_iota(jnp.int32, (32, 64), 0) + 32 * core
    col = lax.broadcasted_iota(jnp.int32, (32, 64), 1)
    pick = (col == (row % MB) * MB + row // MB).astype(F32).astype(BF16)
    lane = lax.broadcasted_iota(jnp.int32, (4, 128), 1)
    line = lax.broadcasted_iota(jnp.int32, (4, 128), 0)
    coeff_copy.wait()
    own = jnp.dot(pick, coeff[0], preferred_element_type=F32)
    own = jnp.concatenate([own[:16], own[16:]], axis=1).astype(BF16)
    list_copy.wait()
    index = jnp.zeros((4, 128), jnp.int32)
    for j in range(4):
        index = jnp.where((lane == place) & (line == j), listed[0, j], index)
    index = index.astype(F32).astype(BF16)
    each = NDEV // PACK_PARTS
    out_copies = []
    for g in range(PACK_PARTS):
        field_copies[g].wait()
        for i in range(g * each, g * each + each):
            for tt in range(2):
                for part in range(2):
                    at = (2 * i + tt) * 128
                    out[i, 2 * tt + part] = field[part, 0, :, at : at + 128]
            for q in range(4):
                out[i, 4 + q] = own[4 * q : 4 * q + 4]
            out[i, 8] = index
        receivers = pl.ds(g * each, each)
        out_copies.append(
            pltpu.make_async_copy(out.at[receivers], out_hbm.at[receivers], out_sems.at[g])
        )
        out_copies[g].start()
    for copy in out_copies:
        copy.wait()


def pack(block_list, field, coeff):
    shape = (NDEV, 9, 4, 128)
    return pl.pallas_call(
        pack_kernel,
        out_shape=jax.ShapeDtypeStruct(shape, BF16),
        in_specs=[in_hbm(), in_hbm(), in_hbm()],
        out_specs=in_hbm(),
        scratch_shapes=[
            pltpu.SMEM(block_list.shape, jnp.int32),
            pltpu.VMEM(field.shape, BF16),
            pltpu.VMEM(coeff.shape, BF16),
            pltpu.VMEM(shape, BF16),
            pltpu.SemaphoreType.DMA((2 + PACK_PARTS,)),
            pltpu.SemaphoreType.DMA((PACK_PARTS,)),
        ],
        compiler_params=params(60 * 2**20),
        name="pack",
    )(block_list, field, coeff)


def kerr_kernel(data_ref, coeff_ref, out_ref, field, total, listed, indices, sem):
    index = jnp.sum(data_ref[:, 8].astype(F32), axis=0)
    listed[...] = jnp.concatenate([index, index], axis=0).astype(jnp.int32)
    list_copy = pltpu.make_async_copy(listed, indices, sem)
    list_copy.start()
    for b in range(NMB):
        for tt in range(2):
            for part in range(2):
                both = jnp.concatenate(
                    [
                        data_ref[2 * b, 2 * tt + part].astype(F32),
                        data_ref[2 * b + 1, 2 * tt + part].astype(F32),
                    ],
                    axis=0,
                )
                field[part, b, :, tt * 128 : tt * 128 + 128] = both
                total[part, b, :, tt * 128 : tt * 128 + 128] = both
    list_copy.wait()

    def one_block(k, carry):
        at_p = indices[0, k]
        at_l = indices[1, k]
        at_m = indices[2, k]
        at_n = indices[3, k]
        n_re = field[0, at_n]
        n_im = field[1, at_n]
        pair_re = []
        pair_im = []
        for m in range(MB):
            m_re = field[0, at_m, m : m + 1, :]
            m_im = field[1, at_m, m : m + 1, :]
            pair_re.append(m_re * n_re + m_im * n_im)
            pair_im.append(m_im * n_re - m_re * n_im)
        pairs = jnp.concatenate(
            [jnp.concatenate(pair_re, axis=0), jnp.concatenate(pair_im, axis=0)], axis=1
        ).astype(BF16)
        low = coeff_ref[0, k]
        high = coeff_ref[1, k]
        table = jnp.concatenate(
            [low[:, :64], low[:, 64:], high[:, :64], high[:, 64:]], axis=0
        )
        weighted = jnp.dot(table, pairs, preferred_element_type=F32)
        term_re = jnp.zeros((MB, 256), F32)
        term_im = jnp.zeros((MB, 256), F32)
        for l in range(MB):
            w_re = weighted[8 * l : 8 * l + 8, :256]
            w_im = weighted[8 * l : 8 * l + 8, 256:]
            l_re = field[0, at_l, l : l + 1, :]
            l_im = field[1, at_l, l : l + 1, :]
            term_re = term_re + (w_re * l_re - w_im * l_im)
            term_im = term_im + (w_re * l_im + w_im * l_re)
        total[0, at_p] -= kerr_strength * term_im
        total[1, at_p] += kerr_strength * term_re
        return carry

    lax.fori_loop(0, NBLK, one_block, 0, unroll=16)

    for b in range(NMB):
        new = (total[0, b], total[1, b])
        for half in range(2):
            pieces = []
            for tt in range(2):
                for part in range(2):
                    pieces.append(
                        new[part][4 * half : 4 * half + 4, tt * 128 : tt * 128 + 128]
                    )
            out_ref[2 * b + half] = jnp.concatenate(pieces, axis=0).astype(BF16)


def kerr_step(data, coeff):
    return pl.pallas_call(
        kerr_kernel,
        out_shape=jax.ShapeDtypeStruct((NDEV, 16, 128), BF16),
        in_specs=[in_vmem(), in_vmem()],
        out_specs=in_vmem(),
        scratch_shapes=[
            pltpu.VMEM((2, NMB, MB, 256), F32),
            pltpu.VMEM((2, NMB, MB, 256), F32),
            pltpu.VMEM((8, 128), jnp.int32),
            pltpu.SMEM((8, 128), jnp.int32),
            pltpu.SemaphoreType.DMA,
        ],
        compiler_params=params(),
        name="kerr",
    )(data, coeff)


def dft_tables():
    a = np.arange(FT)
    angle = 2.0 * math.pi / FT * ((a[:, None] * a[None, :]) % FT)
    cos, sin = np.cos(angle), -np.sin(angle)
    first = np.block([[cos, -sin], [sin, cos]])
    small = 2.0 * math.pi / (FT * FT) * (a[:, None] * a[None, :])
    twist = np.stack([np.cos(small), -np.sin(small)])
    return (
        jnp.asarray(first, BF16),
        jnp.asarray(first / FT, BF16),
        jnp.asarray(twist, F32),
    )


def dft_kernel(first_ref, second_ref, twist_ref, data_ref, out_ref, rows):
    rows[...] = data_ref[...].astype(F32).reshape(1024, 128)
    columns = []
    for m in range(4):
        columns.append(
            jnp.concatenate(
                [rows[pl.ds(m, 128, stride=8), :], rows[pl.ds(4 + m, 128, stride=8), :]],
                axis=0,
            ).astype(BF16)
        )
    half = jnp.dot(
        first_ref[...], jnp.concatenate(columns, axis=1), preferred_element_type=F32
    )
    t_re = twist_ref[0]
    t_im = twist_ref[1]
    turned = []
    for m in range(4):
        h_re = half[:128, 128 * m : 128 * m + 128]
        h_im = half[128:, 128 * m : 128 * m + 128]
        turned.append(
            jnp.concatenate(
                [h_re * t_re - h_im * t_im, h_re * t_im + h_im * t_re], axis=1
            ).astype(BF16)
        )
    spectrum = lax.dot_general(
        second_ref[...],
        jnp.concatenate(turned, axis=0),
        (((1,), (1,)), ((), ())),
        preferred_element_type=F32,
    )
    for part in range(2):
        for m in range(4):
            rows[pl.ds(4 * part + m, 128, stride=8), :] = spectrum[
                128 * part : 128 * part + 128, 128 * m : 128 * m + 128
            ]
    out_ref[...] = rows[...].reshape(NDEV, 16, 128).astype(BF16)


def transform(data):
    first, second, twist = dft_tables()
    return pl.pallas_call(
        dft_kernel,
        out_shape=jax.ShapeDtypeStruct((NDEV, 16, 128), BF16),
        in_specs=[in_vmem()] * 4,
        out_specs=in_vmem(),
        scratch_shapes=[pltpu.VMEM((1024, 128), F32)],
        compiler_params=params(),
        name="dft",
    )(first, second, twist, data)


def order_kernel(data_ref, out_ref):
    for b in range(MODES // 16):
        group = [data_ref[4 * b + s].astype(F32) for s in range(4)]
        for h in range(2):
            for part in range(2):
                at = 8 * h + 4 * part
                piece = jnp.concatenate([g[at : at + 4] for g in group], axis=0).astype(BF16)
                for copy in range(4):
                    out_ref[copy, h, part, 16 * b : 16 * b + 16, :] = piece


def order(data):
    return pl.pallas_call(
        order_kernel,
        out_shape=jax.ShapeDtypeStruct((4, 2, 2, MODES, 128), BF16),
        in_specs=[in_vmem()],
        out_specs=in_vmem(),
        compiler_params=params(),
        name="order",
    )(data)


def gram_kernel(data_ref, own_ref, send_ref):
    core = lax.axis_index("c")
    chip = lax.axis_index("x")
    keep = pl.multiple_of(64 * chip + 32 * core, 32)
    give = pl.multiple_of(64 * chip + 32 * (1 - core), 32)
    lane = lax.broadcasted_iota(jnp.int32, (32, 128), 1) // FB
    for h in range(2):
        lefts = [[] for _ in range(16)]
        rights = []
        for x in range(4):
            rights += [data_ref[x, h, 0], data_ref[x, h, 1]]
            for side, start in enumerate((keep, give)):
                row_re = data_ref[x, h, 0, pl.ds(start, 32), :].astype(F32)
                row_im = data_ref[x, h, 1, pl.ds(start, 32), :].astype(F32)
                for band in range(4):
                    b_re = jnp.where(lane == band, row_re, 0.0)
                    b_im = jnp.where(lane == band, row_im, 0.0)
                    at = 8 * side + 2 * band
                    lefts[at] += [b_re.astype(BF16), b_im.astype(BF16)]
                    lefts[at + 1] += [b_im.astype(BF16), (-b_re).astype(BF16)]
        left = jnp.concatenate([jnp.concatenate(p, axis=1) for p in lefts], axis=0)
        right = jnp.concatenate(rights, axis=1)
        result = lax.dot_general(
            left, right, (((1,), (1,)), ((), ())), preferred_element_type=F32
        ) * (1.0 / 256.0)
        for band in range(4):
            for d in range(2):
                at = 64 * band + 32 * d
                own_ref[4 * h + band, d] = result[at : at + 32]
                send_ref[4 * h + band, d] = result[256 + at : 256 + at + 32].astype(BF16)


def gram(data):
    return pl.pallas_call(
        gram_kernel,
        out_shape=(
            jax.ShapeDtypeStruct((8, 2, 32, MODES), F32),
            jax.ShapeDtypeStruct((8, 2, 32, MODES), BF16),
        ),
        in_specs=[in_vmem()],
        out_specs=(in_vmem(), in_vmem()),
        compiler_params=params(),
        name="gram",
    )(data)


def add_kernel(own_ref, sent_ref, out_hbm, out, sems):
    other = 1 - lax.axis_index("c")
    copies = []
    for b in range(4):
        bands = pl.ds(2 * b, 2)
        out[bands] = own_ref[bands] + sent_ref[other, bands].astype(F32)
        copies.append(pltpu.make_async_copy(out.at[bands], out_hbm.at[bands], sems.at[b]))
        copies[b].start()
    for copy in copies:
        copy.wait()


def add(own, sent):
    return pl.pallas_call(
        add_kernel,
        out_shape=jax.ShapeDtypeStruct(own.shape, F32),
        in_specs=[in_vmem(), in_vmem()],
        out_specs=in_hbm(),
        scratch_shapes=[pltpu.VMEM(own.shape, F32), pltpu.SemaphoreType.DMA((4,))],
        compiler_params=params(),
        name="add",
    )(own, sent)


def swap(array, axes):
    return lax.all_to_all(array, axes, split_axis=0, concat_axis=0, tiled=True)


def shards(input_field, kerr_coeff, block_list):
    timed = swap(pack(block_list, input_field, kerr_coeff), MODE)
    halves = timed[:, 4:8].reshape(NDEV, 16, 128)
    coeff = lax.all_gather(halves, "c", axis=0, tiled=False)
    stepped = kerr_step(timed, coeff)
    spectrum = transform(swap(stepped, MODE))
    banded = order(swap(spectrum, MODE))
    own, send = gram(swap(banded, ("x",)))
    return add(own, lax.all_gather(send, "c", axis=0, tiled=False))


def solution(mesh):
    finer = Mesh(mesh.devices.reshape(8, 8, 4, 2), ("y", "z", "x", "c"))
    return jax.shard_map(
        shards,
        mesh=finer,
        in_specs=(P(None, ("x", "c"), MODE, None), P(MODE, None, None), P(MODE, None)),
        out_specs=P(MODE, None, ("x", "c"), None),
        check_vma=False,
    )
```

```python
import math

import jax
import jax.numpy as jnp
import numpy as np
from jax import lax
from jax.experimental import pallas as pl
from jax.experimental.pallas import tpu as pltpu
from jax.sharding import Mesh
from jax.sharding import PartitionSpec as P

MB = 8
FT = 128
FB = 32
NT = 16384
PACK_PARTS = 4
NMB = 32
NBLK = 64
MODES = 256
NDEV = 64
MODE = ("y", "z")
F32 = jnp.float32
BF16 = jnp.bfloat16

kerr_strength = 0.25

VMEM_LIMIT = 48 * 2**20


def params(limit=VMEM_LIMIT):
    return pltpu.CompilerParams(vmem_limit_bytes=limit)


def in_vmem():
    return pl.BlockSpec(memory_space=pltpu.VMEM)


def in_hbm():
    return pl.BlockSpec(memory_space=pltpu.HBM)


def pack_kernel(list_hbm, field_hbm, coeff_hbm, out_hbm, listed, field, coeff, out, sems, out_sems):
    coeff_copy = pltpu.make_async_copy(coeff_hbm, coeff, sems.at[0])
    list_copy = pltpu.make_async_copy(list_hbm, listed, sems.at[1])
    coeff_copy.start()
    list_copy.start()
    field_copies = []
    for g in range(PACK_PARTS):
        times = pl.ds(g * (NT // PACK_PARTS), NT // PACK_PARTS)
        field_copies.append(
            pltpu.make_async_copy(
                field_hbm.at[:, :, :, times], field.at[:, :, :, times], sems.at[2 + g]
            )
        )
        field_copies[g].start()
    core = lax.axis_index("c")
    place = lax.axis_index(MODE)
    row = lax.broadcasted_iota(jnp.int32, (32, 64), 0) + 32 * core
    col = lax.broadcasted_iota(jnp.int32, (32, 64), 1)
    pick = (col == (row % MB) * MB + row // MB).astype(F32).astype(BF16)
    lane = lax.broadcasted_iota(jnp.int32, (2, 128), 1)
    line = lax.broadcasted_iota(jnp.int32, (2, 128), 0)
    coeff_copy.wait()
    own = jnp.dot(pick, coeff[0], preferred_element_type=F32)
    own = jnp.concatenate([own[:16], own[16:]], axis=1).astype(BF16)
    list_copy.wait()
    index = jnp.zeros((2, 128), jnp.int32)
    for j in range(4):
        here = (lane == place + 64 * (j % 2)) & (line == j // 2)
        index = jnp.where(here, listed[0, j], index)
    index = index.astype(F32).astype(BF16)
    each = NDEV // PACK_PARTS
    out_copies = []
    for g in range(PACK_PARTS):
        field_copies[g].wait()
        for i in range(g * each, g * each + each):
            for tt in range(2):
                for part in range(2):
                    at = (2 * i + tt) * 128
                    tile = field[part, 0, :, at : at + 128]
                    out[i, 4 * tt + 2 * part] = tile[0:2]
                    out[i, 4 * tt + 2 * part + 1] = tile[2:4]
            for q in range(8):
                out[i, 8 + q] = own[2 * q : 2 * q + 2]
            out[i, 16] = index
        receivers = pl.ds(g * each, each)
        out_copies.append(
            pltpu.make_async_copy(out.at[receivers], out_hbm.at[receivers], out_sems.at[g])
        )
        out_copies[g].start()
    for copy in out_copies:
        copy.wait()


def pack(block_list, field, coeff):
    shape = (NDEV, 17, 2, 128)
    return pl.pallas_call(
        pack_kernel,
        out_shape=jax.ShapeDtypeStruct(shape, BF16),
        in_specs=[in_hbm(), in_hbm(), in_hbm()],
        out_specs=in_hbm(),
        scratch_shapes=[
            pltpu.SMEM(block_list.shape, jnp.int32),
            pltpu.VMEM(field.shape, BF16),
            pltpu.VMEM(coeff.shape, BF16),
            pltpu.VMEM(shape, BF16),
            pltpu.SemaphoreType.DMA((2 + PACK_PARTS,)),
            pltpu.SemaphoreType.DMA((PACK_PARTS,)),
        ],
        compiler_params=params(60 * 2**20),
        name="pack",
    )(block_list, field, coeff)


def kerr_kernel(data_ref, coeff_ref, out_ref, field, total):
    index = jnp.sum(data_ref[:, 16].astype(F32), axis=0).astype(jnp.int32)
    for b in range(NMB):
        for tt in range(2):
            for part in range(2):
                at = 4 * tt + 2 * part
                both = jnp.concatenate(
                    [
                        data_ref[2 * b + s, at + h].astype(F32)
                        for s in range(2)
                        for h in range(2)
                    ],
                    axis=0,
                )
                field[part, b, :, tt * 128 : tt * 128 + 128] = both
                total[part, b, :, tt * 128 : tt * 128 + 128] = both

    for k in range(NBLK):
        at_p = index[0, k]
        at_l = index[0, 64 + k]
        at_m = index[1, k]
        at_n = index[1, 64 + k]
        n_re = field[0, at_n]
        n_im = field[1, at_n]
        pair_re = []
        pair_im = []
        for m in range(MB):
            m_re = field[0, at_m, m : m + 1, :]
            m_im = field[1, at_m, m : m + 1, :]
            pair_re.append(m_re * n_re + m_im * n_im)
            pair_im.append(m_im * n_re - m_re * n_im)
        pairs = jnp.concatenate(
            [jnp.concatenate(pair_re, axis=0), jnp.concatenate(pair_im, axis=0)], axis=1
        ).astype(BF16)
        low = coeff_ref[0, k]
        high = coeff_ref[1, k]
        table = jnp.concatenate(
            [low[:, :64], low[:, 64:], high[:, :64], high[:, 64:]], axis=0
        )
        weighted = jnp.dot(table, pairs, preferred_element_type=F32)
        term_re = jnp.zeros((MB, 256), F32)
        term_im = jnp.zeros((MB, 256), F32)
        for l in range(MB):
            w_re = weighted[8 * l : 8 * l + 8, :256]
            w_im = weighted[8 * l : 8 * l + 8, 256:]
            l_re = field[0, at_l, l : l + 1, :]
            l_im = field[1, at_l, l : l + 1, :]
            term_re = term_re + (w_re * l_re - w_im * l_im)
            term_im = term_im + (w_re * l_im + w_im * l_re)
        total[0, at_p] -= kerr_strength * term_im
        total[1, at_p] += kerr_strength * term_re

    for b in range(NMB):
        new = (total[0, b], total[1, b])
        for half in range(2):
            pieces = []
            for tt in range(2):
                for part in range(2):
                    pieces.append(
                        new[part][4 * half : 4 * half + 4, tt * 128 : tt * 128 + 128]
                    )
            out_ref[2 * b + half] = jnp.concatenate(pieces, axis=0).astype(BF16)


def kerr_step(data, coeff):
    return pl.pallas_call(
        kerr_kernel,
        out_shape=jax.ShapeDtypeStruct((NDEV, 16, 128), BF16),
        in_specs=[in_vmem(), in_vmem()],
        out_specs=in_vmem(),
        scratch_shapes=[
            pltpu.VMEM((2, NMB, MB, 256), F32),
            pltpu.VMEM((2, NMB, MB, 256), F32),
        ],
        compiler_params=params(),
        name="kerr",
    )(data, coeff)


def dft_tables():
    a = np.arange(FT)
    angle = 2.0 * math.pi / FT * ((a[:, None] * a[None, :]) % FT)
    cos, sin = np.cos(angle), -np.sin(angle)
    first = np.block([[cos, -sin], [sin, cos]])
    small = 2.0 * math.pi / (FT * FT) * (a[:, None] * a[None, :])
    twist = np.stack([np.cos(small), -np.sin(small)])
    return (
        jnp.asarray(first, BF16),
        jnp.asarray(first / FT, BF16),
        jnp.asarray(twist, F32),
    )


def dft_kernel(first_ref, second_ref, twist_ref, data_ref, out_ref, rows):
    rows[...] = data_ref[...].astype(F32).reshape(1024, 128)
    columns = []
    for m in range(4):
        columns.append(
            jnp.concatenate(
                [rows[pl.ds(m, 128, stride=8), :], rows[pl.ds(4 + m, 128, stride=8), :]],
                axis=0,
            ).astype(BF16)
        )
    half = jnp.dot(
        first_ref[...], jnp.concatenate(columns, axis=1), preferred_element_type=F32
    )
    t_re = twist_ref[0]
    t_im = twist_ref[1]
    turned = []
    for m in range(4):
        h_re = half[:128, 128 * m : 128 * m + 128]
        h_im = half[128:, 128 * m : 128 * m + 128]
        turned.append(
            jnp.concatenate(
                [h_re * t_re - h_im * t_im, h_re * t_im + h_im * t_re], axis=1
            ).astype(BF16)
        )
    spectrum = lax.dot_general(
        second_ref[...],
        jnp.concatenate(turned, axis=0),
        (((1,), (1,)), ((), ())),
        preferred_element_type=F32,
    )
    for part in range(2):
        for m in range(4):
            rows[pl.ds(4 * part + m, 128, stride=8), :] = spectrum[
                128 * part : 128 * part + 128, 128 * m : 128 * m + 128
            ]
    out_ref[...] = rows[...].reshape(NDEV, 16, 128).astype(BF16)


def transform(data):
    first, second, twist = dft_tables()
    return pl.pallas_call(
        dft_kernel,
        out_shape=jax.ShapeDtypeStruct((NDEV, 16, 128), BF16),
        in_specs=[in_vmem()] * 4,
        out_specs=in_vmem(),
        scratch_shapes=[pltpu.VMEM((1024, 128), F32)],
        compiler_params=params(),
        name="dft",
    )(first, second, twist, data)


def order_kernel(data_ref, out_ref):
    for b in range(MODES // 16):
        group = [data_ref[4 * b + s].astype(F32) for s in range(4)]
        for h in range(2):
            for part in range(2):
                at = 8 * h + 4 * part
                piece = jnp.concatenate([g[at : at + 4] for g in group], axis=0).astype(BF16)
                for copy in range(4):
                    out_ref[copy, h, part, 16 * b : 16 * b + 16, :] = piece


def order(data):
    return pl.pallas_call(
        order_kernel,
        out_shape=jax.ShapeDtypeStruct((4, 2, 2, MODES, 128), BF16),
        in_specs=[in_vmem()],
        out_specs=in_vmem(),
        compiler_params=params(),
        name="order",
    )(data)


def gram_kernel(data_ref, own_ref, send_ref):
    core = lax.axis_index("c")
    chip = lax.axis_index("x")
    keep = pl.multiple_of(64 * chip + 32 * core, 32)
    give = pl.multiple_of(64 * chip + 32 * (1 - core), 32)
    lane = lax.broadcasted_iota(jnp.int32, (32, 128), 1) // FB
    for h in range(2):
        lefts = [[] for _ in range(16)]
        rights = []
        for x in range(4):
            rights += [data_ref[x, h, 0], data_ref[x, h, 1]]
            for side, start in enumerate((keep, give)):
                row_re = data_ref[x, h, 0, pl.ds(start, 32), :].astype(F32)
                row_im = data_ref[x, h, 1, pl.ds(start, 32), :].astype(F32)
                for band in range(4):
                    b_re = jnp.where(lane == band, row_re, 0.0)
                    b_im = jnp.where(lane == band, row_im, 0.0)
                    at = 8 * side + 2 * band
                    lefts[at] += [b_re.astype(BF16), b_im.astype(BF16)]
                    lefts[at + 1] += [b_im.astype(BF16), (-b_re).astype(BF16)]
        left = jnp.concatenate([jnp.concatenate(p, axis=1) for p in lefts], axis=0)
        right = jnp.concatenate(rights, axis=1)
        result = lax.dot_general(
            left, right, (((1,), (1,)), ((), ())), preferred_element_type=F32
        ) * (1.0 / 256.0)
        for band in range(4):
            for d in range(2):
                at = 64 * band + 32 * d
                own_ref[4 * h + band, d] = result[at : at + 32]
                send_ref[4 * h + band, d] = result[256 + at : 256 + at + 32].astype(BF16)


def gram(data):
    return pl.pallas_call(
        gram_kernel,
        out_shape=(
            jax.ShapeDtypeStruct((8, 2, 32, MODES), F32),
            jax.ShapeDtypeStruct((8, 2, 32, MODES), BF16),
        ),
        in_specs=[in_vmem()],
        out_specs=(in_vmem(), in_vmem()),
        compiler_params=params(),
        name="gram",
    )(data)


def add_kernel(own_ref, sent_ref, out_hbm, out, sems):
    other = 1 - lax.axis_index("c")
    copies = []
    for b in range(4):
        bands = pl.ds(2 * b, 2)
        out[bands] = own_ref[bands] + sent_ref[other, bands].astype(F32)
        copies.append(pltpu.make_async_copy(out.at[bands], out_hbm.at[bands], sems.at[b]))
        copies[b].start()
    for copy in copies:
        copy.wait()


def add(own, sent):
    return pl.pallas_call(
        add_kernel,
        out_shape=jax.ShapeDtypeStruct(own.shape, F32),
        in_specs=[in_vmem(), in_vmem()],
        out_specs=in_hbm(),
        scratch_shapes=[pltpu.VMEM(own.shape, F32), pltpu.SemaphoreType.DMA((4,))],
        compiler_params=params(),
        name="add",
    )(own, sent)


def swap(array, axes):
    return lax.all_to_all(array, axes, split_axis=0, concat_axis=0, tiled=True)


def shards(input_field, kerr_coeff, block_list):
    timed = swap(pack(block_list, input_field, kerr_coeff), MODE)
    halves = timed[:, 8:16].reshape(NDEV, 16, 128)
    coeff = lax.all_gather(halves, "c", axis=0, tiled=False)
    stepped = kerr_step(timed, coeff)
    spectrum = transform(swap(stepped, MODE))
    banded = order(swap(spectrum, MODE))
    own, send = gram(swap(banded, ("x",)))
    return add(own, lax.all_gather(send, "c", axis=0, tiled=False))


def solution(mesh):
    finer = Mesh(mesh.devices.reshape(8, 8, 4, 2), ("y", "z", "x", "c"))
    return jax.shard_map(
        shards,
        mesh=finer,
        in_specs=(P(None, ("x", "c"), MODE, None), P(MODE, None, None), P(MODE, None)),
        out_specs=P(MODE, None, ("x", "c"), None),
        check_vma=False,
    )
```

```python
import math

import jax
import jax.numpy as jnp
import numpy as np
from jax import lax
from jax.experimental import pallas as pl
from jax.experimental.pallas import tpu as pltpu
from jax.sharding import Mesh
from jax.sharding import PartitionSpec as P

MB = 8
FT = 128
FB = 32
NT = 16384
PACK_PARTS = 4
NMB = 32
NBLK = 64
MODES = 256
NDEV = 64
MODE = ("y", "z")
F32 = jnp.float32
BF16 = jnp.bfloat16

kerr_strength = 0.25

VMEM_LIMIT = 48 * 2**20


def params(limit=VMEM_LIMIT):
    return pltpu.CompilerParams(vmem_limit_bytes=limit)


def in_vmem():
    return pl.BlockSpec(memory_space=pltpu.VMEM)


def in_hbm():
    return pl.BlockSpec(memory_space=pltpu.HBM)


def pack_kernel(list_hbm, field_hbm, coeff_hbm, out_hbm, listed, field, coeff, out, sems, out_sems):
    coeff_copy = pltpu.make_async_copy(coeff_hbm, coeff, sems.at[0])
    list_copy = pltpu.make_async_copy(list_hbm, listed, sems.at[1])
    coeff_copy.start()
    list_copy.start()
    field_copies = []
    for g in range(PACK_PARTS):
        times = pl.ds(g * (NT // PACK_PARTS), NT // PACK_PARTS)
        field_copies.append(
            pltpu.make_async_copy(
                field_hbm.at[:, :, :, times], field.at[:, :, :, times], sems.at[2 + g]
            )
        )
        field_copies[g].start()
    core = lax.axis_index("c")
    place = lax.axis_index(MODE)
    row = lax.broadcasted_iota(jnp.int32, (32, 64), 0) + 32 * core
    col = lax.broadcasted_iota(jnp.int32, (32, 64), 1)
    pick = (col == (row % MB) * MB + row // MB).astype(F32).astype(BF16)
    lane = lax.broadcasted_iota(jnp.int32, (2, 128), 1)
    line = lax.broadcasted_iota(jnp.int32, (2, 128), 0)
    coeff_copy.wait()
    own = jnp.dot(pick, coeff[0], preferred_element_type=F32)
    own = jnp.concatenate([own[:16], own[16:]], axis=1).astype(BF16)
    list_copy.wait()
    index = jnp.zeros((2, 128), jnp.int32)
    for j in range(4):
        here = (lane == place + 64 * (j % 2)) & (line == j // 2)
        index = jnp.where(here, listed[0, j], index)
    index = index.astype(F32).astype(BF16)
    each = NDEV // PACK_PARTS
    out_copies = []
    for g in range(PACK_PARTS):
        field_copies[g].wait()
        for i in range(g * each, g * each + each):
            for tt in range(2):
                for part in range(2):
                    at = (2 * i + tt) * 128
                    tile = field[part, 0, :, at : at + 128]
                    out[i, 4 * tt + 2 * part] = tile[0:2]
                    out[i, 4 * tt + 2 * part + 1] = tile[2:4]
            for q in range(8):
                out[i, 8 + q] = own[2 * q : 2 * q + 2]
            out[i, 16] = index
        receivers = pl.ds(g * each, each)
        out_copies.append(
            pltpu.make_async_copy(out.at[receivers], out_hbm.at[receivers], out_sems.at[g])
        )
        out_copies[g].start()
    for copy in out_copies:
        copy.wait()


def pack(block_list, field, coeff):
    shape = (NDEV, 17, 2, 128)
    return pl.pallas_call(
        pack_kernel,
        out_shape=jax.ShapeDtypeStruct(shape, BF16),
        in_specs=[in_hbm(), in_hbm(), in_hbm()],
        out_specs=in_hbm(),
        scratch_shapes=[
            pltpu.SMEM(block_list.shape, jnp.int32),
            pltpu.VMEM(field.shape, BF16),
            pltpu.VMEM(coeff.shape, BF16),
            pltpu.VMEM(shape, BF16),
            pltpu.SemaphoreType.DMA((2 + PACK_PARTS,)),
            pltpu.SemaphoreType.DMA((PACK_PARTS,)),
        ],
        compiler_params=params(60 * 2**20),
        name="pack",
    )(block_list, field, coeff)


def kerr_kernel(data_ref, coeff_ref, out_ref, spread, twice, total):
    index = jnp.sum(data_ref[:, 16].astype(F32), axis=0).astype(jnp.int32)
    for b in range(NMB):
        for tt in range(2):
            times = slice(tt * 128, tt * 128 + 128)
            for part in range(2):
                at = 4 * tt + 2 * part
                both = jnp.concatenate(
                    [
                        data_ref[2 * b + s, at + h].astype(F32)
                        for s in range(2)
                        for h in range(2)
                    ],
                    axis=0,
                )
                total[part, b, :, times] = both
                twice[part, b, :, times] = jnp.concatenate([both, both], axis=0).astype(BF16)
                for j in range(4):
                    spread[part, b, j, :, times] = jnp.concatenate(
                        [
                            jnp.broadcast_to(both[2 * j + h : 2 * j + h + 1], (8, 128))
                            for h in range(2)
                        ],
                        axis=0,
                    ).astype(BF16)

    for k in range(NBLK):
        at_p = index[0, k]
        at_l = index[0, 64 + k]
        at_m = index[1, k]
        at_n = index[1, 64 + k]
        n_re = twice[0, at_n]
        n_im = twice[1, at_n]
        pair_re = []
        pair_im = []
        for j in range(4):
            m_re = spread[0, at_m, j]
            m_im = spread[1, at_m, j]
            pair_re.append(m_re * n_re + m_im * n_im)
            pair_im.append(m_im * n_re - m_re * n_im)
        pairs = jnp.concatenate(
            [jnp.concatenate(pair_re, axis=0), jnp.concatenate(pair_im, axis=0)], axis=1
        )
        low = coeff_ref[0, k]
        high = coeff_ref[1, k]
        table = jnp.concatenate(
            [low[:, :64], low[:, 64:], high[:, :64], high[:, 64:]], axis=0
        )
        weighted = jnp.dot(table, pairs, preferred_element_type=F32)
        weighted = weighted.astype(BF16)
        term_re = None
        for j in range(4):
            w_re = weighted[16 * j : 16 * j + 16, :256]
            w_im = weighted[16 * j : 16 * j + 16, 256:]
            l_re = spread[0, at_l, j]
            l_im = spread[1, at_l, j]
            one_re = w_re * l_re - w_im * l_im
            one_im = w_re * l_im + w_im * l_re
            term_re = one_re if j == 0 else term_re + one_re
            term_im = one_im if j == 0 else term_im + one_im
        term_re = term_re.astype(F32)
        term_im = term_im.astype(F32)
        total[0, at_p] -= kerr_strength * (term_im[:8] + term_im[8:])
        total[1, at_p] += kerr_strength * (term_re[:8] + term_re[8:])

    for b in range(NMB):
        new = (total[0, b], total[1, b])
        for half in range(2):
            pieces = []
            for tt in range(2):
                for part in range(2):
                    pieces.append(
                        new[part][4 * half : 4 * half + 4, tt * 128 : tt * 128 + 128]
                    )
            out_ref[2 * b + half] = jnp.concatenate(pieces, axis=0).astype(BF16)


def kerr_step(data, coeff):
    return pl.pallas_call(
        kerr_kernel,
        out_shape=jax.ShapeDtypeStruct((NDEV, 16, 128), BF16),
        in_specs=[in_vmem(), in_vmem()],
        out_specs=in_vmem(),
        scratch_shapes=[
            pltpu.VMEM((2, NMB, 4, 16, 256), BF16),
            pltpu.VMEM((2, NMB, 16, 256), BF16),
            pltpu.VMEM((2, NMB, MB, 256), F32),
        ],
        compiler_params=params(),
        name="kerr",
    )(data, coeff)


def dft_tables():
    a = np.arange(FT)
    angle = 2.0 * math.pi / FT * ((a[:, None] * a[None, :]) % FT)
    cos, sin = np.cos(angle), -np.sin(angle)
    first = np.block([[cos, -sin], [sin, cos]])
    small = 2.0 * math.pi / (FT * FT) * (a[:, None] * a[None, :])
    twist = np.stack([np.cos(small), -np.sin(small)])
    return (
        jnp.asarray(first, BF16),
        jnp.asarray(first / FT, BF16),
        jnp.asarray(twist, F32),
    )


def dft_kernel(first_ref, second_ref, twist_ref, data_ref, out_ref, rows):
    rows[...] = data_ref[...].astype(F32).reshape(1024, 128)
    columns = []
    for m in range(4):
        columns.append(
            jnp.concatenate(
                [rows[pl.ds(m, 128, stride=8), :], rows[pl.ds(4 + m, 128, stride=8), :]],
                axis=0,
            ).astype(BF16)
        )
    half = jnp.dot(
        first_ref[...], jnp.concatenate(columns, axis=1), preferred_element_type=F32
    )
    t_re = twist_ref[0]
    t_im = twist_ref[1]
    turned = []
    for m in range(4):
        h_re = half[:128, 128 * m : 128 * m + 128]
        h_im = half[128:, 128 * m : 128 * m + 128]
        turned.append(
            jnp.concatenate(
                [h_re * t_re - h_im * t_im, h_re * t_im + h_im * t_re], axis=1
            ).astype(BF16)
        )
    spectrum = lax.dot_general(
        second_ref[...],
        jnp.concatenate(turned, axis=0),
        (((1,), (1,)), ((), ())),
        preferred_element_type=F32,
    )
    for part in range(2):
        for m in range(4):
            rows[pl.ds(4 * part + m, 128, stride=8), :] = spectrum[
                128 * part : 128 * part + 128, 128 * m : 128 * m + 128
            ]
    out_ref[...] = rows[...].reshape(NDEV, 16, 128).astype(BF16)


def transform(data):
    first, second, twist = dft_tables()
    return pl.pallas_call(
        dft_kernel,
        out_shape=jax.ShapeDtypeStruct((NDEV, 16, 128), BF16),
        in_specs=[in_vmem()] * 4,
        out_specs=in_vmem(),
        scratch_shapes=[pltpu.VMEM((1024, 128), F32)],
        compiler_params=params(),
        name="dft",
    )(first, second, twist, data)


def order_kernel(data_ref, out_ref):
    for b in range(MODES // 16):
        group = [data_ref[4 * b + s].astype(F32) for s in range(4)]
        for h in range(2):
            for part in range(2):
                at = 8 * h + 4 * part
                piece = jnp.concatenate([g[at : at + 4] for g in group], axis=0).astype(BF16)
                for copy in range(4):
                    out_ref[copy, h, part, 16 * b : 16 * b + 16, :] = piece


def order(data):
    return pl.pallas_call(
        order_kernel,
        out_shape=jax.ShapeDtypeStruct((4, 2, 2, MODES, 128), BF16),
        in_specs=[in_vmem()],
        out_specs=in_vmem(),
        compiler_params=params(),
        name="order",
    )(data)


def gram_kernel(data_ref, own_ref, send_ref):
    core = lax.axis_index("c")
    chip = lax.axis_index("x")
    keep = pl.multiple_of(64 * chip + 32 * core, 32)
    give = pl.multiple_of(64 * chip + 32 * (1 - core), 32)
    lane = lax.broadcasted_iota(jnp.int32, (32, 128), 1) // FB
    for h in range(2):
        lefts = [[] for _ in range(16)]
        rights = []
        for x in range(4):
            rights += [data_ref[x, h, 0], data_ref[x, h, 1]]
            for side, start in enumerate((keep, give)):
                row_re = data_ref[x, h, 0, pl.ds(start, 32), :].astype(F32)
                row_im = data_ref[x, h, 1, pl.ds(start, 32), :].astype(F32)
                for band in range(4):
                    b_re = jnp.where(lane == band, row_re, 0.0)
                    b_im = jnp.where(lane == band, row_im, 0.0)
                    at = 8 * side + 2 * band
                    lefts[at] += [b_re.astype(BF16), b_im.astype(BF16)]
                    lefts[at + 1] += [b_im.astype(BF16), (-b_re).astype(BF16)]
        left = jnp.concatenate([jnp.concatenate(p, axis=1) for p in lefts], axis=0)
        right = jnp.concatenate(rights, axis=1)
        result = lax.dot_general(
            left, right, (((1,), (1,)), ((), ())), preferred_element_type=F32
        ) * (1.0 / 256.0)
        for band in range(4):
            for d in range(2):
                at = 64 * band + 32 * d
                own_ref[4 * h + band, d] = result[at : at + 32]
                send_ref[4 * h + band, d] = result[256 + at : 256 + at + 32].astype(BF16)


def gram(data):
    return pl.pallas_call(
        gram_kernel,
        out_shape=(
            jax.ShapeDtypeStruct((8, 2, 32, MODES), F32),
            jax.ShapeDtypeStruct((8, 2, 32, MODES), BF16),
        ),
        in_specs=[in_vmem()],
        out_specs=(in_vmem(), in_vmem()),
        compiler_params=params(),
        name="gram",
    )(data)


def add_kernel(own_ref, sent_ref, out_hbm, out, sems):
    other = 1 - lax.axis_index("c")
    copies = []
    for b in range(4):
        bands = pl.ds(2 * b, 2)
        out[bands] = own_ref[bands] + sent_ref[other, bands].astype(F32)
        copies.append(pltpu.make_async_copy(out.at[bands], out_hbm.at[bands], sems.at[b]))
        copies[b].start()
    for copy in copies:
        copy.wait()


def add(own, sent):
    return pl.pallas_call(
        add_kernel,
        out_shape=jax.ShapeDtypeStruct(own.shape, F32),
        in_specs=[in_vmem(), in_vmem()],
        out_specs=in_hbm(),
        scratch_shapes=[pltpu.VMEM(own.shape, F32), pltpu.SemaphoreType.DMA((4,))],
        compiler_params=params(),
        name="add",
    )(own, sent)


def swap(array, axes):
    return lax.all_to_all(array, axes, split_axis=0, concat_axis=0, tiled=True)


def shards(input_field, kerr_coeff, block_list):
    timed = swap(pack(block_list, input_field, kerr_coeff), MODE)
    halves = timed[:, 8:16].reshape(NDEV, 16, 128)
    coeff = lax.all_gather(halves, "c", axis=0, tiled=False)
    stepped = kerr_step(timed, coeff)
    spectrum = transform(swap(stepped, MODE))
    banded = order(swap(spectrum, MODE))
    own, send = gram(swap(banded, ("x",)))
    return add(own, lax.all_gather(send, "c", axis=0, tiled=False))


def solution(mesh):
    finer = Mesh(mesh.devices.reshape(8, 8, 4, 2), ("y", "z", "x", "c"))
    return jax.shard_map(
        shards,
        mesh=finer,
        in_specs=(P(None, ("x", "c"), MODE, None), P(MODE, None, None), P(MODE, None)),
        out_specs=P(MODE, None, ("x", "c"), None),
        check_vma=False,
    )
```

```python
import math

import jax
import jax.numpy as jnp
import numpy as np
from jax import lax
from jax.experimental import pallas as pl
from jax.experimental.pallas import tpu as pltpu
from jax.sharding import Mesh
from jax.sharding import PartitionSpec as P

MB = 8
FT = 128
FB = 32
NMB = 32
NBLK = 64
MODES = 256
NDEV = 64
MODE = ("y", "z")
F32 = jnp.float32
BF16 = jnp.bfloat16

kerr_strength = 0.25

VMEM_LIMIT = 48 * 2**20


def params(limit=VMEM_LIMIT):
    return pltpu.CompilerParams(vmem_limit_bytes=limit)


def in_vmem():
    return pl.BlockSpec(memory_space=pltpu.VMEM)


def in_hbm():
    return pl.BlockSpec(memory_space=pltpu.HBM)


def pick_kernel(out_ref):
    row = lax.broadcasted_iota(jnp.int32, (32, 64), 0) + 32 * lax.axis_index("c")
    col = lax.broadcasted_iota(jnp.int32, (32, 64), 1)
    out_ref[...] = (col == (row % MB) * MB + row // MB).astype(F32).astype(BF16)


def pick():
    return pl.pallas_call(
        pick_kernel,
        out_shape=jax.ShapeDtypeStruct((32, 64), BF16),
        out_specs=in_vmem(),
        compiler_params=params(),
        cost_estimate=pl.CostEstimate(
            flops=2 * 10**9, bytes_accessed=2**20, transcendentals=0
        ),
        name="pick",
    )()


def pack_kernel(pick_ref, list_ref, field_ref, coeff_ref, out_ref):
    place = lax.axis_index(MODE)
    own = jnp.dot(pick_ref[...], coeff_ref[0], preferred_element_type=F32)
    own = jnp.concatenate([own[:16], own[16:]], axis=1).astype(BF16)
    lane = lax.broadcasted_iota(jnp.int32, (2, 128), 1)
    line = lax.broadcasted_iota(jnp.int32, (2, 128), 0)
    index = jnp.zeros((2, 128), jnp.int32)
    for j in range(4):
        here = (lane == place + 64 * (j % 2)) & (line == j // 2)
        index = jnp.where(here, list_ref[0:1, j : j + 1], index)
    index = index.astype(F32).astype(BF16)
    for i in range(NDEV):
        for tt in range(2):
            for part in range(2):
                at = (2 * i + tt) * 128
                tile = field_ref[part, 0, :, at : at + 128]
                out_ref[i, 4 * tt + 2 * part] = tile[0:2]
                out_ref[i, 4 * tt + 2 * part + 1] = tile[2:4]
        for q in range(8):
            out_ref[i, 8 + q] = own[2 * q : 2 * q + 2]
        out_ref[i, 16] = index


def pack(block_list, field, coeff):
    return pl.pallas_call(
        pack_kernel,
        out_shape=jax.ShapeDtypeStruct((NDEV, 17, 2, 128), BF16),
        in_specs=[in_vmem()] * 4,
        out_specs=in_vmem(),
        compiler_params=params(),
        name="pack",
    )(pick(), block_list, field, coeff)


def kerr_kernel(data_ref, coeff_ref, out_ref, spread, twice, total):
    index = jnp.sum(data_ref[:, 16].astype(F32), axis=0).astype(jnp.int32)
    for b in range(NMB):
        for tt in range(2):
            times = slice(tt * 128, tt * 128 + 128)
            for part in range(2):
                at = 4 * tt + 2 * part
                both = jnp.concatenate(
                    [
                        data_ref[2 * b + s, at + h].astype(F32)
                        for s in range(2)
                        for h in range(2)
                    ],
                    axis=0,
                )
                total[part, b, :, times] = both
                twice[part, b, :, times] = jnp.concatenate([both, both], axis=0).astype(BF16)
                for j in range(4):
                    spread[part, b, j, :, times] = jnp.concatenate(
                        [
                            jnp.broadcast_to(both[2 * j + h : 2 * j + h + 1], (8, 128))
                            for h in range(2)
                        ],
                        axis=0,
                    ).astype(BF16)

    for k in range(NBLK):
        at_p = index[0, k]
        at_l = index[0, 64 + k]
        at_m = index[1, k]
        at_n = index[1, 64 + k]
        n_re = twice[0, at_n]
        n_im = twice[1, at_n]
        pair_re = []
        pair_im = []
        for j in range(4):
            m_re = spread[0, at_m, j]
            m_im = spread[1, at_m, j]
            pair_re.append(m_re * n_re + m_im * n_im)
            pair_im.append(m_im * n_re - m_re * n_im)
        pairs = jnp.concatenate(
            [jnp.concatenate(pair_re, axis=0), jnp.concatenate(pair_im, axis=0)], axis=1
        )
        low = coeff_ref[0, k]
        high = coeff_ref[1, k]
        table = jnp.concatenate(
            [low[:, :64], low[:, 64:], high[:, :64], high[:, 64:]], axis=0
        )
        weighted = jnp.dot(table, pairs, preferred_element_type=F32)
        weighted = weighted.astype(BF16)
        term_re = None
        for j in range(4):
            w_re = weighted[16 * j : 16 * j + 16, :256]
            w_im = weighted[16 * j : 16 * j + 16, 256:]
            l_re = spread[0, at_l, j]
            l_im = spread[1, at_l, j]
            one_re = w_re * l_re - w_im * l_im
            one_im = w_re * l_im + w_im * l_re
            term_re = one_re if j == 0 else term_re + one_re
            term_im = one_im if j == 0 else term_im + one_im
        term_re = term_re.astype(F32)
        term_im = term_im.astype(F32)
        total[0, at_p] -= kerr_strength * (term_im[:8] + term_im[8:])
        total[1, at_p] += kerr_strength * (term_re[:8] + term_re[8:])

    for b in range(NMB):
        new = (total[0, b], total[1, b])
        for half in range(2):
            pieces = []
            for tt in range(2):
                for part in range(2):
                    pieces.append(
                        new[part][4 * half : 4 * half + 4, tt * 128 : tt * 128 + 128]
                    )
            out_ref[2 * b + half] = jnp.concatenate(pieces, axis=0).astype(BF16)


def kerr_step(data, coeff):
    return pl.pallas_call(
        kerr_kernel,
        out_shape=jax.ShapeDtypeStruct((NDEV, 16, 128), BF16),
        in_specs=[in_vmem(), in_vmem()],
        out_specs=in_vmem(),
        scratch_shapes=[
            pltpu.VMEM((2, NMB, 4, 16, 256), BF16),
            pltpu.VMEM((2, NMB, 16, 256), BF16),
            pltpu.VMEM((2, NMB, MB, 256), F32),
        ],
        compiler_params=params(),
        name="kerr",
    )(data, coeff)


def dft_tables():
    a = np.arange(FT)
    angle = 2.0 * math.pi / FT * ((a[:, None] * a[None, :]) % FT)
    cos, sin = np.cos(angle), -np.sin(angle)
    first = np.block([[cos, -sin], [sin, cos]])
    small = 2.0 * math.pi / (FT * FT) * (a[:, None] * a[None, :])
    twist = np.stack([np.cos(small), -np.sin(small)])
    return (
        jnp.asarray(first, BF16),
        jnp.asarray(first / FT, BF16),
        jnp.asarray(twist, F32),
    )


def dft_kernel(first_ref, second_ref, twist_ref, data_ref, out_ref, rows):
    rows[...] = data_ref[...].astype(F32).reshape(1024, 128)
    columns = []
    for m in range(4):
        columns.append(
            jnp.concatenate(
                [rows[pl.ds(m, 128, stride=8), :], rows[pl.ds(4 + m, 128, stride=8), :]],
                axis=0,
            ).astype(BF16)
        )
    half = jnp.dot(
        first_ref[...], jnp.concatenate(columns, axis=1), preferred_element_type=F32
    )
    t_re = twist_ref[0]
    t_im = twist_ref[1]
    turned = []
    for m in range(4):
        h_re = half[:128, 128 * m : 128 * m + 128]
        h_im = half[128:, 128 * m : 128 * m + 128]
        turned.append(
            jnp.concatenate(
                [h_re * t_re - h_im * t_im, h_re * t_im + h_im * t_re], axis=1
            ).astype(BF16)
        )
    spectrum = lax.dot_general(
        second_ref[...],
        jnp.concatenate(turned, axis=0),
        (((1,), (1,)), ((), ())),
        preferred_element_type=F32,
    )
    for part in range(2):
        for m in range(4):
            rows[pl.ds(4 * part + m, 128, stride=8), :] = spectrum[
                128 * part : 128 * part + 128, 128 * m : 128 * m + 128
            ]
    out_ref[...] = rows[...].reshape(NDEV, 16, 128).astype(BF16)


def transform(data):
    first, second, twist = dft_tables()
    return pl.pallas_call(
        dft_kernel,
        out_shape=jax.ShapeDtypeStruct((NDEV, 16, 128), BF16),
        in_specs=[in_vmem()] * 4,
        out_specs=in_vmem(),
        scratch_shapes=[pltpu.VMEM((1024, 128), F32)],
        compiler_params=params(),
        name="dft",
    )(first, second, twist, data)


def order_kernel(data_ref, out_ref):
    for b in range(MODES // 16):
        group = [data_ref[4 * b + s].astype(F32) for s in range(4)]
        for h in range(2):
            for part in range(2):
                at = 8 * h + 4 * part
                piece = jnp.concatenate([g[at : at + 4] for g in group], axis=0).astype(BF16)
                for copy in range(4):
                    out_ref[copy, h, part, 16 * b : 16 * b + 16, :] = piece


def order(data):
    return pl.pallas_call(
        order_kernel,
        out_shape=jax.ShapeDtypeStruct((4, 2, 2, MODES, 128), BF16),
        in_specs=[in_vmem()],
        out_specs=in_vmem(),
        compiler_params=params(),
        name="order",
    )(data)


def gram_kernel(data_ref, own_ref, send_ref):
    core = lax.axis_index("c")
    chip = lax.axis_index("x")
    keep = pl.multiple_of(64 * chip + 32 * core, 32)
    give = pl.multiple_of(64 * chip + 32 * (1 - core), 32)
    lane = lax.broadcasted_iota(jnp.int32, (32, 128), 1) // FB
    for h in range(2):
        lefts = [[] for _ in range(16)]
        rights = []
        for x in range(4):
            rights += [data_ref[x, h, 0], data_ref[x, h, 1]]
            for side, start in enumerate((keep, give)):
                row_re = data_ref[x, h, 0, pl.ds(start, 32), :].astype(F32)
                row_im = data_ref[x, h, 1, pl.ds(start, 32), :].astype(F32)
                for band in range(4):
                    b_re = jnp.where(lane == band, row_re, 0.0)
                    b_im = jnp.where(lane == band, row_im, 0.0)
                    at = 8 * side + 2 * band
                    lefts[at] += [b_re.astype(BF16), b_im.astype(BF16)]
                    lefts[at + 1] += [b_im.astype(BF16), (-b_re).astype(BF16)]
        left = jnp.concatenate([jnp.concatenate(p, axis=1) for p in lefts], axis=0)
        right = jnp.concatenate(rights, axis=1)
        result = lax.dot_general(
            left, right, (((1,), (1,)), ((), ())), preferred_element_type=F32
        ) * (1.0 / 256.0)
        for band in range(4):
            for d in range(2):
                at = 64 * band + 32 * d
                own_ref[4 * h + band, d] = result[at : at + 32]
                send_ref[4 * h + band, d] = result[256 + at : 256 + at + 32].astype(BF16)


def gram(data):
    return pl.pallas_call(
        gram_kernel,
        out_shape=(
            jax.ShapeDtypeStruct((8, 2, 32, MODES), F32),
            jax.ShapeDtypeStruct((8, 2, 32, MODES), BF16),
        ),
        in_specs=[in_vmem()],
        out_specs=(in_vmem(), in_vmem()),
        compiler_params=params(),
        name="gram",
    )(data)


def add_kernel(own_ref, sent_ref, out_hbm, out, sems):
    other = 1 - lax.axis_index("c")
    copies = []
    for b in range(4):
        bands = pl.ds(2 * b, 2)
        out[bands] = own_ref[bands] + sent_ref[other, bands].astype(F32)
        copies.append(pltpu.make_async_copy(out.at[bands], out_hbm.at[bands], sems.at[b]))
        copies[b].start()
    for copy in copies:
        copy.wait()


def add(own, sent):
    return pl.pallas_call(
        add_kernel,
        out_shape=jax.ShapeDtypeStruct(own.shape, F32),
        in_specs=[in_vmem(), in_vmem()],
        out_specs=in_hbm(),
        scratch_shapes=[pltpu.VMEM(own.shape, F32), pltpu.SemaphoreType.DMA((4,))],
        compiler_params=params(),
        name="add",
    )(own, sent)


def swap(array, axes):
    return lax.all_to_all(array, axes, split_axis=0, concat_axis=0, tiled=True)


def shards(input_field, kerr_coeff, block_list):
    timed = swap(pack(block_list, input_field, kerr_coeff), MODE)
    halves = timed[:, 8:16].reshape(NDEV, 16, 128)
    coeff = lax.all_gather(halves, "c", axis=0, tiled=False)
    stepped = kerr_step(timed, coeff)
    spectrum = transform(swap(stepped, MODE))
    banded = order(swap(spectrum, MODE))
    own, send = gram(swap(banded, ("x",)))
    return add(own, lax.all_gather(send, "c", axis=0, tiled=False))


def solution(mesh):
    finer = Mesh(mesh.devices.reshape(8, 8, 4, 2), ("y", "z", "x", "c"))
    return jax.shard_map(
        shards,
        mesh=finer,
        in_specs=(P(None, ("x", "c"), MODE, None), P(MODE, None, None), P(MODE, None)),
        out_specs=P(MODE, None, ("x", "c"), None),
        check_vma=False,
    )
```

```python
import math

import jax
import jax.numpy as jnp
import numpy as np
from jax import lax
from jax.experimental import pallas as pl
from jax.experimental.pallas import tpu as pltpu
from jax.sharding import Mesh
from jax.sharding import PartitionSpec as P

MB = 8
FT = 128
FB = 32
NMB = 32
NBLK = 64
MODES = 256
NDEV = 64
MODE = ("y", "z")
F32 = jnp.float32
BF16 = jnp.bfloat16

kerr_strength = 0.25

VMEM_LIMIT = 48 * 2**20


def params(limit=VMEM_LIMIT):
    return pltpu.CompilerParams(vmem_limit_bytes=limit)


def in_vmem():
    return pl.BlockSpec(memory_space=pltpu.VMEM)


def in_hbm():
    return pl.BlockSpec(memory_space=pltpu.HBM)


def pick_kernel(out_ref):
    row = lax.broadcasted_iota(jnp.int32, (32, 64), 0) + 32 * lax.axis_index("c")
    col = lax.broadcasted_iota(jnp.int32, (32, 64), 1)
    own = (col == (row % MB) * MB + row // MB).astype(F32)
    out_ref[...] = (kerr_strength * own).astype(BF16)


def pick():
    return pl.pallas_call(
        pick_kernel,
        out_shape=jax.ShapeDtypeStruct((32, 64), BF16),
        out_specs=in_vmem(),
        compiler_params=params(),
        cost_estimate=pl.CostEstimate(
            flops=2 * 10**9, bytes_accessed=2**20, transcendentals=0
        ),
        name="pick",
    )()


def pack_kernel(pick_ref, list_ref, field_ref, coeff_ref, out_ref):
    place = lax.axis_index(MODE)
    own = jnp.dot(pick_ref[...], coeff_ref[0], preferred_element_type=F32)
    own = jnp.concatenate([own[:16], own[16:]], axis=1).astype(BF16)
    lane = lax.broadcasted_iota(jnp.int32, (2, 128), 1)
    line = lax.broadcasted_iota(jnp.int32, (2, 128), 0)
    index = jnp.zeros((2, 128), jnp.int32)
    for j in range(4):
        here = (lane == place + 64 * (j % 2)) & (line == j // 2)
        index = jnp.where(here, list_ref[0:1, j : j + 1], index)
    index = index.astype(F32).astype(BF16)
    for i in range(NDEV):
        for tt in range(2):
            for part in range(2):
                at = (2 * i + tt) * 128
                tile = field_ref[part, 0, :, at : at + 128]
                out_ref[i, 4 * tt + 2 * part] = tile[0:2]
                out_ref[i, 4 * tt + 2 * part + 1] = tile[2:4]
        for q in range(8):
            out_ref[i, 8 + q] = own[2 * q : 2 * q + 2]
        out_ref[i, 16] = index


def pack(block_list, field, coeff):
    return pl.pallas_call(
        pack_kernel,
        out_shape=jax.ShapeDtypeStruct((NDEV, 17, 2, 128), BF16),
        in_specs=[in_vmem()] * 4,
        out_specs=in_vmem(),
        compiler_params=params(),
        name="pack",
    )(pick(), block_list, field, coeff)


def kerr_kernel(data_ref, coeff_ref, out_ref, spread, twice, total):
    index = jnp.sum(data_ref[:, 16].astype(F32), axis=0).astype(jnp.int32)
    for b in range(NMB):
        for tt in range(2):
            times = slice(tt * 128, tt * 128 + 128)
            for part in range(2):
                at = 4 * tt + 2 * part
                both = jnp.concatenate(
                    [
                        data_ref[2 * b + s, at + h].astype(F32)
                        for s in range(2)
                        for h in range(2)
                    ],
                    axis=0,
                )
                total[part, b, :, times] = both
                twice[part, b, :, times] = jnp.concatenate([both, both], axis=0).astype(BF16)
                for j in range(4):
                    spread[part, b, j, :, times] = jnp.concatenate(
                        [
                            jnp.broadcast_to(both[2 * j + h : 2 * j + h + 1], (8, 128))
                            for h in range(2)
                        ],
                        axis=0,
                    ).astype(BF16)

    for k in range(NBLK):
        at_p = index[0, k]
        at_l = index[0, 64 + k]
        at_m = index[1, k]
        at_n = index[1, 64 + k]
        n_re = twice[0, at_n]
        n_im = twice[1, at_n]
        pair_re = []
        pair_im = []
        for j in range(4):
            m_re = spread[0, at_m, j]
            m_im = spread[1, at_m, j]
            pair_re.append(m_re * n_re + m_im * n_im)
            pair_im.append(m_im * n_re - m_re * n_im)
        pairs = jnp.concatenate(
            [jnp.concatenate(pair_re, axis=0), jnp.concatenate(pair_im, axis=0)], axis=1
        )
        low = coeff_ref[0, k]
        high = coeff_ref[1, k]
        table = jnp.concatenate(
            [low[:, :64], low[:, 64:], high[:, :64], high[:, 64:]], axis=0
        )
        weighted = jnp.dot(table, pairs, preferred_element_type=F32)
        weighted = weighted.astype(BF16)
        term_re = None
        for j in range(4):
            w_re = weighted[16 * j : 16 * j + 16, :256]
            w_im = weighted[16 * j : 16 * j + 16, 256:]
            l_re = spread[0, at_l, j]
            l_im = spread[1, at_l, j]
            one_re = w_re * l_re - w_im * l_im
            one_im = w_re * l_im + w_im * l_re
            term_re = one_re if j == 0 else term_re + one_re
            term_im = one_im if j == 0 else term_im + one_im
        term_re = term_re.astype(F32)
        term_im = term_im.astype(F32)
        total[0, at_p] -= term_im[:8] + term_im[8:]
        total[1, at_p] += term_re[:8] + term_re[8:]

    for b in range(NMB):
        new = (total[0, b], total[1, b])
        for half in range(2):
            pieces = []
            for tt in range(2):
                for part in range(2):
                    pieces.append(
                        new[part][4 * half : 4 * half + 4, tt * 128 : tt * 128 + 128]
                    )
            out_ref[2 * b + half] = jnp.concatenate(pieces, axis=0).astype(BF16)


def kerr_step(data, coeff):
    return pl.pallas_call(
        kerr_kernel,
        out_shape=jax.ShapeDtypeStruct((NDEV, 16, 128), BF16),
        in_specs=[in_vmem(), in_vmem()],
        out_specs=in_vmem(),
        scratch_shapes=[
            pltpu.VMEM((2, NMB, 4, 16, 256), BF16),
            pltpu.VMEM((2, NMB, 16, 256), BF16),
            pltpu.VMEM((2, NMB, MB, 256), F32),
        ],
        compiler_params=params(),
        name="kerr",
    )(data, coeff)


def dft_tables():
    a = np.arange(FT)
    angle = 2.0 * math.pi / FT * ((a[:, None] * a[None, :]) % FT)
    cos, sin = np.cos(angle), -np.sin(angle)
    first = np.block([[cos, -sin], [sin, cos]])
    small = 2.0 * math.pi / (FT * FT) * (a[:, None] * a[None, :])
    twist = np.stack([np.cos(small), -np.sin(small)])
    return (
        jnp.asarray(first, BF16),
        jnp.asarray(first / FT, BF16),
        jnp.asarray(twist, F32),
    )


def dft_kernel(first_ref, second_ref, twist_ref, data_ref, out_ref, rows):
    rows[...] = data_ref[...].astype(F32).reshape(1024, 128)
    columns = []
    for m in range(4):
        columns.append(
            jnp.concatenate(
                [rows[pl.ds(m, 128, stride=8), :], rows[pl.ds(4 + m, 128, stride=8), :]],
                axis=0,
            ).astype(BF16)
        )
    half = jnp.dot(
        first_ref[...], jnp.concatenate(columns, axis=1), preferred_element_type=F32
    )
    t_re = twist_ref[0]
    t_im = twist_ref[1]
    turned = []
    for m in range(4):
        h_re = half[:128, 128 * m : 128 * m + 128]
        h_im = half[128:, 128 * m : 128 * m + 128]
        turned.append(
            jnp.concatenate(
                [h_re * t_re - h_im * t_im, h_re * t_im + h_im * t_re], axis=1
            ).astype(BF16)
        )
    spectrum = lax.dot_general(
        second_ref[...],
        jnp.concatenate(turned, axis=0),
        (((1,), (1,)), ((), ())),
        preferred_element_type=F32,
    )
    for part in range(2):
        for m in range(4):
            rows[pl.ds(4 * part + m, 128, stride=8), :] = spectrum[
                128 * part : 128 * part + 128, 128 * m : 128 * m + 128
            ]
    out_ref[...] = rows[...].reshape(NDEV, 16, 128).astype(BF16)


def transform(data):
    first, second, twist = dft_tables()
    return pl.pallas_call(
        dft_kernel,
        out_shape=jax.ShapeDtypeStruct((NDEV, 16, 128), BF16),
        in_specs=[in_vmem()] * 4,
        out_specs=in_vmem(),
        scratch_shapes=[pltpu.VMEM((1024, 128), F32)],
        compiler_params=params(),
        name="dft",
    )(first, second, twist, data)


def order_kernel(data_ref, out_ref):
    for b in range(MODES // 16):
        group = [data_ref[4 * b + s].astype(F32) for s in range(4)]
        for h in range(2):
            for part in range(2):
                at = 8 * h + 4 * part
                piece = jnp.concatenate([g[at : at + 4] for g in group], axis=0).astype(BF16)
                for copy in range(4):
                    out_ref[copy, h, part, 16 * b : 16 * b + 16, :] = piece


def order(data):
    return pl.pallas_call(
        order_kernel,
        out_shape=jax.ShapeDtypeStruct((4, 2, 2, MODES, 128), BF16),
        in_specs=[in_vmem()],
        out_specs=in_vmem(),
        compiler_params=params(),
        name="order",
    )(data)


def gram_kernel(data_ref, own_ref, send_ref):
    core = lax.axis_index("c")
    chip = lax.axis_index("x")
    keep = pl.multiple_of(64 * chip + 32 * core, 32)
    give = pl.multiple_of(64 * chip + 32 * (1 - core), 32)
    lane = lax.broadcasted_iota(jnp.int32, (32, 128), 1) // FB
    ones = [(lane == band).astype(F32) for band in range(4)]
    minus = [(-one).astype(BF16) for one in ones]
    ones = [one.astype(BF16) for one in ones]
    for h in range(2):
        lefts = [[] for _ in range(16)]
        rights = []
        for x in range(4):
            rights += [data_ref[x, h, 0], data_ref[x, h, 1]]
            for side, start in enumerate((keep, give)):
                row_re = data_ref[x, h, 0, pl.ds(start, 32), :]
                row_im = data_ref[x, h, 1, pl.ds(start, 32), :]
                for band in range(4):
                    at = 8 * side + 2 * band
                    b_im = row_im * ones[band]
                    lefts[at] += [row_re * ones[band], b_im]
                    lefts[at + 1] += [b_im, row_re * minus[band]]
        left = jnp.concatenate([jnp.concatenate(p, axis=1) for p in lefts], axis=0)
        right = jnp.concatenate(rights, axis=1)
        result = lax.dot_general(
            left, right, (((1,), (1,)), ((), ())), preferred_element_type=F32
        ) * (1.0 / 256.0)
        for band in range(4):
            for d in range(2):
                at = 64 * band + 32 * d
                own_ref[4 * h + band, d] = result[at : at + 32]
                send_ref[4 * h + band, d] = result[256 + at : 256 + at + 32].astype(BF16)


def gram(data):
    return pl.pallas_call(
        gram_kernel,
        out_shape=(
            jax.ShapeDtypeStruct((8, 2, 32, MODES), F32),
            jax.ShapeDtypeStruct((8, 2, 32, MODES), BF16),
        ),
        in_specs=[in_vmem()],
        out_specs=(in_vmem(), in_vmem()),
        compiler_params=params(),
        name="gram",
    )(data)


def add_kernel(own_ref, sent_ref, out_hbm, out, sems):
    other = 1 - lax.axis_index("c")
    copies = []
    for b in range(4):
        bands = pl.ds(2 * b, 2)
        out[bands] = own_ref[bands] + sent_ref[other, bands].astype(F32)
        copies.append(pltpu.make_async_copy(out.at[bands], out_hbm.at[bands], sems.at[b]))
        copies[b].start()
    for copy in copies:
        copy.wait()


def add(own, sent):
    return pl.pallas_call(
        add_kernel,
        out_shape=jax.ShapeDtypeStruct(own.shape, F32),
        in_specs=[in_vmem(), in_vmem()],
        out_specs=in_hbm(),
        scratch_shapes=[pltpu.VMEM(own.shape, F32), pltpu.SemaphoreType.DMA((4,))],
        compiler_params=params(),
        name="add",
    )(own, sent)


def swap(array, axes):
    return lax.all_to_all(array, axes, split_axis=0, concat_axis=0, tiled=True)


def shards(input_field, kerr_coeff, block_list):
    timed = swap(pack(block_list, input_field, kerr_coeff), MODE)
    halves = timed[:, 8:16].reshape(NDEV, 16, 128)
    coeff = lax.all_gather(halves, "c", axis=0, tiled=False)
    stepped = kerr_step(timed, coeff)
    spectrum = transform(swap(stepped, MODE))
    banded = order(swap(spectrum, MODE))
    own, send = gram(swap(banded, ("x",)))
    return add(own, lax.all_gather(send, "c", axis=0, tiled=False))


def solution(mesh):
    finer = Mesh(mesh.devices.reshape(8, 8, 4, 2), ("y", "z", "x", "c"))
    return jax.shard_map(
        shards,
        mesh=finer,
        in_specs=(P(None, ("x", "c"), MODE, None), P(MODE, None, None), P(MODE, None)),
        out_specs=P(MODE, None, ("x", "c"), None),
        check_vma=False,
    )
```

```python
import math

import jax
import jax.numpy as jnp
import numpy as np
from jax import lax
from jax.experimental import pallas as pl
from jax.experimental.pallas import tpu as pltpu
from jax.sharding import Mesh
from jax.sharding import PartitionSpec as P

MB = 8
FT = 128
FB = 32
NMB = 32
NBLK = 64
MODES = 256
NDEV = 64
MODE = ("y", "z")
F32 = jnp.float32
BF16 = jnp.bfloat16

kerr_strength = 0.25

VMEM_LIMIT = 48 * 2**20


def params(limit=VMEM_LIMIT):
    return pltpu.CompilerParams(vmem_limit_bytes=limit)


def in_vmem():
    return pl.BlockSpec(memory_space=pltpu.VMEM)


def in_hbm():
    return pl.BlockSpec(memory_space=pltpu.HBM)


def pick_kernel(out_ref):
    row = lax.broadcasted_iota(jnp.int32, (32, 64), 0) + 32 * lax.axis_index("c")
    col = lax.broadcasted_iota(jnp.int32, (32, 64), 1)
    own = (col == (row % MB) * MB + row // MB).astype(F32)
    out_ref[...] = (kerr_strength * own).astype(BF16)


def pick():
    return pl.pallas_call(
        pick_kernel,
        out_shape=jax.ShapeDtypeStruct((32, 64), BF16),
        out_specs=in_vmem(),
        compiler_params=params(),
        cost_estimate=pl.CostEstimate(
            flops=2 * 10**9, bytes_accessed=2**20, transcendentals=0
        ),
        name="pick",
    )()


def pack_kernel(pick_ref, list_ref, field_ref, coeff_ref, out_ref):
    place = lax.axis_index(MODE)
    own = jnp.dot(pick_ref[...], coeff_ref[0], preferred_element_type=F32)
    own = jnp.concatenate([own[:16], own[16:]], axis=1).astype(BF16)
    lane = lax.broadcasted_iota(jnp.int32, (2, 128), 1)
    line = lax.broadcasted_iota(jnp.int32, (2, 128), 0)
    index = jnp.zeros((2, 128), jnp.int32)
    for j in range(4):
        here = (lane == place + 64 * (j % 2)) & (line == j // 2)
        index = jnp.where(here, list_ref[0:1, j : j + 1], index)
    index = index.astype(F32).astype(BF16)
    for i in range(NDEV):
        for tt in range(2):
            for part in range(2):
                at = (2 * i + tt) * 128
                tile = field_ref[part, 0, :, at : at + 128]
                out_ref[i, 4 * tt + 2 * part] = tile[0:2]
                out_ref[i, 4 * tt + 2 * part + 1] = tile[2:4]
        for q in range(8):
            out_ref[i, 8 + q] = own[2 * q : 2 * q + 2]
        out_ref[i, 16] = index


def pack(block_list, field, coeff):
    return pl.pallas_call(
        pack_kernel,
        out_shape=jax.ShapeDtypeStruct((NDEV, 17, 2, 128), BF16),
        in_specs=[in_vmem()] * 4,
        out_specs=in_vmem(),
        compiler_params=params(),
        name="pack",
    )(pick(), block_list, field, coeff)


def kerr_kernel(data_ref, coeff_ref, out_ref, spread, twice, total):
    index = jnp.sum(data_ref[:, 16].astype(F32), axis=0).astype(jnp.int32)
    for b in range(NMB):
        for tt in range(2):
            times = slice(tt * 128, tt * 128 + 128)
            for part in range(2):
                at = 4 * tt + 2 * part
                both = jnp.concatenate(
                    [
                        data_ref[2 * b + s, at + h].astype(F32)
                        for s in range(2)
                        for h in range(2)
                    ],
                    axis=0,
                )
                total[part, b, :, times] = both
                twice[part, b, :, times] = jnp.concatenate([both, both], axis=0).astype(BF16)
                for j in range(4):
                    spread[part, b, j, :, times] = jnp.concatenate(
                        [
                            jnp.broadcast_to(both[2 * j + h : 2 * j + h + 1], (8, 128))
                            for h in range(2)
                        ],
                        axis=0,
                    ).astype(BF16)

    for k in range(NBLK):
        at_p = index[0, k]
        at_l = index[0, 64 + k]
        at_m = index[1, k]
        at_n = index[1, 64 + k]
        n_re = twice[0, at_n]
        n_im = twice[1, at_n]
        pair_re = []
        pair_im = []
        for j in range(4):
            m_re = spread[0, at_m, j]
            m_im = spread[1, at_m, j]
            pair_re.append(m_re * n_re + m_im * n_im)
            pair_im.append(m_im * n_re - m_re * n_im)
        pairs = jnp.concatenate(
            [jnp.concatenate(pair_re, axis=0), jnp.concatenate(pair_im, axis=0)], axis=1
        )
        low = coeff_ref[0, k]
        high = coeff_ref[1, k]
        table = jnp.concatenate(
            [low[:, :64], low[:, 64:], high[:, :64], high[:, 64:]], axis=0
        )
        weighted = jnp.dot(table, pairs, preferred_element_type=F32)
        weighted = weighted.astype(BF16)
        term_re = None
        for j in range(4):
            w_re = weighted[16 * j : 16 * j + 16, :256]
            w_im = weighted[16 * j : 16 * j + 16, 256:]
            l_re = spread[0, at_l, j]
            l_im = spread[1, at_l, j]
            one_re = w_re * l_re - w_im * l_im
            one_im = w_re * l_im + w_im * l_re
            term_re = one_re if j == 0 else term_re + one_re
            term_im = one_im if j == 0 else term_im + one_im
        term_re = term_re.astype(F32)
        term_im = term_im.astype(F32)
        total[0, at_p] -= term_im[:8] + term_im[8:]
        total[1, at_p] += term_re[:8] + term_re[8:]

    for b in range(NMB):
        new = (total[0, b], total[1, b])
        for half in range(2):
            pieces = []
            for tt in range(2):
                for part in range(2):
                    pieces.append(
                        new[part][4 * half : 4 * half + 4, tt * 128 : tt * 128 + 128]
                    )
            out_ref[2 * b + half] = jnp.concatenate(pieces, axis=0).astype(BF16)


def kerr_step(data, coeff):
    return pl.pallas_call(
        kerr_kernel,
        out_shape=jax.ShapeDtypeStruct((NDEV, 16, 128), BF16),
        in_specs=[in_vmem(), in_vmem()],
        out_specs=in_vmem(),
        scratch_shapes=[
            pltpu.VMEM((2, NMB, 4, 16, 256), BF16),
            pltpu.VMEM((2, NMB, 16, 256), BF16),
            pltpu.VMEM((2, NMB, MB, 256), F32),
        ],
        compiler_params=params(),
        name="kerr",
    )(data, coeff)


def dft_tables():
    a = np.arange(FT)
    angle = 2.0 * math.pi / FT * ((a[:, None] * a[None, :]) % FT)
    cos, sin = np.cos(angle), -np.sin(angle)
    first = np.block([[cos, -sin], [sin, cos]])
    small = 2.0 * math.pi / (FT * FT) * (a[:, None] * a[None, :])
    twist = np.stack([np.cos(small), -np.sin(small)])
    return (
        jnp.asarray(first, BF16),
        jnp.asarray(first / FT, BF16),
        jnp.asarray(twist, F32),
    )


def dft_kernel(first_ref, second_ref, twist_ref, data_ref, out_ref, rows):
    rows[...] = data_ref[...].astype(F32).reshape(1024, 128)
    columns = []
    for m in range(4):
        columns.append(
            jnp.concatenate(
                [rows[pl.ds(m, 128, stride=8), :], rows[pl.ds(4 + m, 128, stride=8), :]],
                axis=0,
            ).astype(BF16)
        )
    half = jnp.dot(
        first_ref[...], jnp.concatenate(columns, axis=1), preferred_element_type=F32
    )
    t_re = twist_ref[0]
    t_im = twist_ref[1]
    turned = []
    for m in range(4):
        h_re = half[:128, 128 * m : 128 * m + 128]
        h_im = half[128:, 128 * m : 128 * m + 128]
        turned.append(
            jnp.concatenate(
                [h_re * t_re - h_im * t_im, h_re * t_im + h_im * t_re], axis=1
            ).astype(BF16)
        )
    spectrum = lax.dot_general(
        second_ref[...],
        jnp.concatenate(turned, axis=0),
        (((1,), (1,)), ((), ())),
        preferred_element_type=F32,
    )
    for part in range(2):
        for m in range(4):
            rows[pl.ds(4 * part + m, 128, stride=8), :] = spectrum[
                128 * part : 128 * part + 128, 128 * m : 128 * m + 128
            ]
    out_ref[...] = rows[...].reshape(NDEV, 16, 128).astype(BF16)


def transform(data):
    first, second, twist = dft_tables()
    return pl.pallas_call(
        dft_kernel,
        out_shape=jax.ShapeDtypeStruct((NDEV, 16, 128), BF16),
        in_specs=[in_vmem()] * 4,
        out_specs=in_vmem(),
        scratch_shapes=[pltpu.VMEM((1024, 128), F32)],
        compiler_params=params(),
        name="dft",
    )(first, second, twist, data)


def order_kernel(data_ref, out_ref):
    for b in range(MODES // 16):
        group = [data_ref[4 * b + s].astype(F32) for s in range(4)]
        for h in range(2):
            for part in range(2):
                at = 8 * h + 4 * part
                piece = jnp.concatenate([g[at : at + 4] for g in group], axis=0).astype(BF16)
                for copy in range(4):
                    out_ref[copy, h, part, 16 * b : 16 * b + 16, :] = piece


def order(data):
    return pl.pallas_call(
        order_kernel,
        out_shape=jax.ShapeDtypeStruct((4, 2, 2, MODES, 128), BF16),
        in_specs=[in_vmem()],
        out_specs=in_vmem(),
        compiler_params=params(),
        name="order",
    )(data)


def gram_kernel(data_ref, own_ref, send_ref):
    core = lax.axis_index("c")
    chip = lax.axis_index("x")
    keep = pl.multiple_of(64 * chip + 32 * core, 32)
    give = pl.multiple_of(64 * chip + 32 * (1 - core), 32)
    lane = lax.broadcasted_iota(jnp.int32, (32, 128), 1) // FB
    for h in range(2):
        lefts = [[] for _ in range(16)]
        rights = []
        for x in range(4):
            rights += [data_ref[x, h, 0], data_ref[x, h, 1]]
            for side, start in enumerate((keep, give)):
                row_re = data_ref[x, h, 0, pl.ds(start, 32), :].astype(F32)
                row_im = data_ref[x, h, 1, pl.ds(start, 32), :].astype(F32)
                for band in range(4):
                    b_re = jnp.where(lane == band, row_re, 0.0)
                    b_im = jnp.where(lane == band, row_im, 0.0)
                    at = 8 * side + 2 * band
                    lefts[at] += [b_re.astype(BF16), b_im.astype(BF16)]
                    lefts[at + 1] += [b_im.astype(BF16), (-b_re).astype(BF16)]
        left = jnp.concatenate([jnp.concatenate(p, axis=1) for p in lefts], axis=0)
        right = jnp.concatenate(rights, axis=1)
        result = lax.dot_general(
            left, right, (((1,), (1,)), ((), ())), preferred_element_type=F32
        ) * (1.0 / 256.0)
        for band in range(4):
            for d in range(2):
                at = 64 * band + 32 * d
                own_ref[4 * h + band, d] = result[at : at + 32]
                send_ref[4 * h + band, d] = result[256 + at : 256 + at + 32].astype(BF16)


def gram(data):
    return pl.pallas_call(
        gram_kernel,
        out_shape=(
            jax.ShapeDtypeStruct((8, 2, 32, MODES), F32),
            jax.ShapeDtypeStruct((8, 2, 32, MODES), BF16),
        ),
        in_specs=[in_vmem()],
        out_specs=(in_vmem(), in_vmem()),
        compiler_params=params(),
        name="gram",
    )(data)


def add_kernel(own_ref, sent_ref, out_hbm, out, sems):
    other = 1 - lax.axis_index("c")
    copies = []
    for b in range(4):
        bands = pl.ds(2 * b, 2)
        out[bands] = own_ref[bands] + sent_ref[other, bands].astype(F32)
        copies.append(pltpu.make_async_copy(out.at[bands], out_hbm.at[bands], sems.at[b]))
        copies[b].start()
    for copy in copies:
        copy.wait()


def add(own, sent):
    return pl.pallas_call(
        add_kernel,
        out_shape=jax.ShapeDtypeStruct(own.shape, F32),
        in_specs=[in_vmem(), in_vmem()],
        out_specs=in_hbm(),
        scratch_shapes=[pltpu.VMEM(own.shape, F32), pltpu.SemaphoreType.DMA((4,))],
        compiler_params=params(),
        name="add",
    )(own, sent)


def swap(array, axes):
    return lax.all_to_all(array, axes, split_axis=0, concat_axis=0, tiled=True)


def shards(input_field, kerr_coeff, block_list):
    timed = swap(pack(block_list, input_field, kerr_coeff), MODE)
    halves = timed[:, 8:16].reshape(NDEV, 16, 128)
    coeff = lax.all_gather(halves, "c", axis=0, tiled=False)
    stepped = kerr_step(timed, coeff)
    spectrum = transform(swap(stepped, MODE))
    banded = order(swap(spectrum, MODE))
    own, send = gram(swap(banded, ("x",)))
    return add(own, lax.all_gather(send, "c", axis=0, tiled=False))


def solution(mesh):
    finer = Mesh(mesh.devices.reshape(8, 8, 4, 2), ("y", "z", "x", "c"))
    return jax.shard_map(
        shards,
        mesh=finer,
        in_specs=(P(None, ("x", "c"), MODE, None), P(MODE, None, None), P(MODE, None)),
        out_specs=P(MODE, None, ("x", "c"), None),
        check_vma=False,
    )
```
